256 devices in a mesh: dp: 32 (over y, z_lo, core), shard: 8 (over x, z_hi).
Axes of the slice: x: 4, y: 4, z: 8 (z_hi: 2, z_lo: 4; z = z_hi * 4 + z_lo), core: 2. Of those that a mesh axis runs over, the one named last changes fastest.
Arguments:
- features: bfloat16 [16384, 8192], P('dp', 'shard'), may hold values from -6 to 6
- out_grads: bfloat16 [16384, 28672], P('dp', 'shard'), may hold values from -0.046875 to 0.046875
- proj_basis: bfloat16 [8192, 512], P('shard'), may hold values from -0.0625 to 0.0625
- first_moment: float32 [8, 3584, 512], P('shard', 'dp'), may hold values from -2 to 2
- second_moment: float32 [8, 3584, 512], P('shard', 'dp'), may hold values from 0.02 to 1
Outputs:
- update: bfloat16 [8, 3584, 8192], P(None, 'dp', 'shard')
- first_new: float32 [8, 3584, 512], P('shard', 'dp')
- second_new: float32 [8, 3584, 512], P('shard', 'dp')
The draws below stay inside these ranges and needn't reach their ends.
All inputs are finite; a program needn't handle non-finite values.
Results may differ from the reference program's by a relative error of at most 0.0052.
Values may be sent and summed in bfloat16 or wider, within the bound.
No kernel may reach another device: no remote copies, remote signals or barrier semaphores. Data moves between devices by JAX's collectives and lax.ppermute only.
A program may use at most 64 MiB of HBM per device.

```python
import math
import jax
import jax.numpy as jnp
from jax import lax

D = 8192
FF = 28672
RANK = 512
TOKENS = 16384
FF_SH = 3584
N_SHARD = 8


def raised(values, rng, source, target, parts, factor):
    def block_of(position):
        return (jnp.arange(values.shape[position]) // (values.shape[position] // parts)).reshape((-1,) + (1,) * (values.ndim - 1 - position))

    near = jax.random.permutation(rng, parts)[block_of(target)]
    second = (block_of(target) + parts // 2) % parts
    return jnp.where((block_of(source) == near) | (block_of(source) == second), factor * values, values)


def block_levels(key, extent, shards, low, largest):
    def one(dim, blocks):
        draws = jax.random.uniform(jax.random.fold_in(jax.random.fold_in(key, 6), dim), (blocks,), jnp.float32, low / len(shards), largest / len(shards))
        return jnp.repeat(jnp.exp(draws), extent[dim] // blocks).reshape((-1,) + (1,) * (len(extent) - dim - 1))

    level = one(*shards[0])
    for cut in shards[1:]:
        level = level * one(*cut)
    return level


def bell_draw(stream_key, extent, width, bound, shards=(), kind=jnp.bfloat16):
    entries = width * jax.random.normal(stream_key, extent, jnp.float32)
    if shards:
        entries = entries * block_levels(stream_key, extent, shards, -0.22, 0.18)
    return jnp.clip(entries, -bound, bound).astype(kind)


def bell_draw_with(stream_key, dims, width, most, shards, heavy, dtype=jnp.bfloat16):
    array = width * jax.random.normal(stream_key, dims, jnp.float32)
    if shards:
        array = array * block_levels(stream_key, dims, shards, -0.22, 0.18)
    return jnp.clip(raised(array, jax.random.fold_in(stream_key, 3), *heavy), -most, most).astype(dtype)


def setup_inputs(seed: int = 0) -> dict:
    key_list = jax.random.split(jax.random.key(seed), 6)
    features = bell_draw(key_list[0], (TOKENS, D), 1.0, 6.0, ((0, 32), (1, 8)))
    out_grads = bell_draw_with(key_list[1], (TOKENS, FF), (1.0 / (TOKENS ** 0.5)), 0.046875, ((0, 32), (1, 8)), (0, 1, 32, 2.75))
    proj_basis = bell_draw(key_list[2], (D, RANK), D ** -0.5, 0.0625, ((0, 8),))
    first_moment = bell_draw(key_list[3], (N_SHARD, FF_SH, RANK), 0.3, 2.0, ((0, 8), (1, 32)), jnp.float32)
    second_moment = jnp.clip(jnp.exp(math.log(1.0) - 3.912023 * jax.random.uniform(key_list[4], (N_SHARD, FF_SH, RANK), jnp.float32) ** block_levels(key_list[4], (N_SHARD, FF_SH, RANK), ((0, 8), (1, 32)), -0.2, 0.2)), 0.02, 1.0)
    return dict(features=features, out_grads=out_grads, proj_basis=proj_basis, first_moment=first_moment, second_moment=second_moment)


beta_first = 0.9
beta_second = 0.99
correct_first = 0.9999734386011124
correct_second = 0.6339676587267705
epsilon = 1e-08
galore_scale = 4.0

def reference(features, out_grads, proj_basis, first_moment, second_moment):
    projected = jnp.dot(features, proj_basis, preferred_element_type=jnp.float32).astype(jnp.bfloat16)
    low_grad = lax.dot_general(out_grads, projected, (((0,), (0,)), ((), ())), preferred_element_type=jnp.float32)
    low_grad = low_grad.reshape(N_SHARD, FF // N_SHARD, RANK)
    first_new = beta_first * first_moment + (1.0 - beta_first) * low_grad
    second_new = beta_second * second_moment + (1.0 - beta_second) * low_grad * low_grad
    direction = (first_new / correct_first / (jnp.sqrt(second_new / correct_second) + epsilon)).astype(jnp.bfloat16)
    full_update = jnp.dot(direction.reshape(FF, RANK), proj_basis.T, preferred_element_type=jnp.float32)
    update = (galore_scale * full_update).astype(jnp.bfloat16).reshape(N_SHARD, FF // N_SHARD, D)
    return (update, first_new, second_new)
```

```python
import functools

import jax
import jax.numpy as jnp
from jax import lax
from jax.experimental import pallas as pl
from jax.experimental.pallas import tpu as pltpu
from jax.sharding import PartitionSpec as P

beta_first = 0.9
beta_second = 0.99
correct_first = 0.9999734386011124
correct_second = 0.6339676587267705
epsilon = 1e-08
galore_scale = 4.0

bf16, f32 = jnp.bfloat16, jnp.float32
NY, NZ, NC, NX, NH = 4, 4, 2, 4, 2
VMEM = pl.BlockSpec(memory_space=pltpu.VMEM)
ANY = pl.BlockSpec(memory_space=pl.ANY)


def dp_perm(step):
    pairs = []
    for y in range(NY):
        for z in range(NZ):
            for c in range(NC):
                ty, tz, tc = step(y, z, c)
                pairs.append(((y * NZ + z) * NC + c, ((ty % NY) * NZ + tz) * NC + tc))
    return pairs


def shard_perm(step):
    pairs = []
    for x in range(NX):
        for h in range(NH):
            tx, th = step(x, h)
            pairs.append((x * NH + h, (tx % NX) * NH + th))
    return pairs


def to_core(a):
    return lax.ppermute(a, "dp", dp_perm(lambda y, z, c: (y, z, 1 - c)))


def to_y(a, k):
    return lax.ppermute(a, "dp", dp_perm(lambda y, z, c: (y + k, z, c)))


def to_z(a, k):
    return lax.ppermute(a, "dp", dp_perm(lambda y, z, c: (y, z ^ k, c)))


def to_x(a, k):
    return lax.ppermute(a, "shard", shard_perm(lambda x, h: (x + k, h)))


def to_h(a):
    return lax.ppermute(a, "shard", shard_perm(lambda x, h: (x, 1 - h)))


def place():
    dp, shard = lax.axis_index("dp"), lax.axis_index("shard")
    return dp // (NZ * NC), (dp // NC) % NZ, dp % NC, shard // NH, shard % NH


def call(body, outs, n_in, scratch=(), limit=16, **kw):
    return pl.pallas_call(
        body,
        out_shape=[jax.ShapeDtypeStruct(s, d) for s, d in outs],
        in_specs=kw.pop("in_specs", [VMEM] * n_in),
        out_specs=kw.pop("out_specs", [VMEM] * len(outs)),
        scratch_shapes=list(scratch),
        compiler_params=pltpu.CompilerParams(vmem_limit_bytes=limit << 20),
        **kw,
    )


def project_body(feat, basis, own, s1, s2, s3):
    _, _, _, x, _ = place()
    rows = own.shape[0]
    for k, out in ((2, s2), (1, s1), (3, s3), (0, own)):
        start = pl.multiple_of(lax.rem(x + k, NX) * rows, rows)
        part = jnp.dot(feat[pl.ds(start, rows), :], basis[...], preferred_element_type=f32)
        out[...] = part.astype(out.dtype)


def turn_body(grads, basis, keep, send, basis_t, tmp):
    y, z, c, x, _ = place()
    rows = keep.shape[2]
    wide = NZ * NC * rows
    toks = grads.shape[0] // NX
    for ry in range(NY):
        col = pl.multiple_of(lax.rem(y + ry, NY) * wide, 128)
        for k in range(NX):
            tok = pl.multiple_of(lax.rem(x + NX - k, NX) * toks, toks)
            tmp[:, k * toks : (k + 1) * toks] = grads[pl.ds(tok, toks), pl.ds(col, wide)].T
        for rz in range(NZ):
            for cc, out in ((0, keep), (1, send)):
                start = pl.multiple_of(((z ^ rz) * NC + (c ^ cc)) * rows, 16)
                out[ry, rz] = tmp[pl.ds(start, rows), :]
    basis_t[...] = basis[...].T


def sum_x_body(own, r1, r2, r3, total, sent):
    t = own[...] + r1[...].astype(f32) + r2[...].astype(f32) + r3[...].astype(f32)
    total[...] = t
    sent[...] = t.astype(bf16)


def sum_h_body(own, other, out):
    out[...] = (own[...] + other[...].astype(f32)).astype(bf16)


def low_body(keep, other, p0, p1, p2, p3, q, own, s1, s2, s3):
    pieces = (p0, p1, p2, p3)
    toks = p0.shape[0]
    proj = jnp.concatenate([p[...] for p in pieces], axis=0)
    for ry, out in ((2, s2), (1, s1), (3, s3), (0, own)):
        a = keep[ry].reshape(out.shape[0], NX * toks)
        b = other[ry].reshape(out.shape[0], NX * toks)
        part = jnp.dot(a, proj, preferred_element_type=f32)
        part += jnp.dot(b, q[...], preferred_element_type=f32)
        out[...] = part.astype(out.dtype)


def sum_y_body(own, r1, r2, r3, total, s1, s2, s3):
    rows = total.shape[0]
    for rz, out in ((3, s3), (2, s2), (1, s1), (0, total)):
        part = slice(rz * rows, (rz + 1) * rows)
        t = own[part, :] + r1[part, :].astype(f32) + r2[part, :].astype(f32) + r3[part, :].astype(f32)
        out[...] = t.astype(out.dtype)


def adam_body(own, r1, r2, r3, first, second, first_new, second_new, direction):
    g = own[...] + r1[...].astype(f32) + r2[...].astype(f32) + r3[...].astype(f32)
    m = beta_first * first[0] + (1.0 - beta_first) * g
    v = beta_second * second[0] + (1.0 - beta_second) * g * g
    first_new[0] = m
    second_new[0] = v
    d = m / correct_first / (jnp.sqrt(v / correct_second) + epsilon)
    direction[...] = d.astype(bf16)


def update_body(moves, aliased, *refs):
    n = len(moves)
    dirs, basis_t = refs[:n], refs[n]
    out, buf, sems = refs[n + 1 + aliased :]
    _, _, _, x, h = place()
    copies = []
    for i, (k, flip) in enumerate(moves):
        t = galore_scale * jnp.dot(dirs[i][...], basis_t[...], preferred_element_type=f32)
        buf[i] = t.astype(bf16)
        block = lax.rem(x + NX - k, NX) * NH + (h ^ flip)
        copy = pltpu.make_async_copy(buf.at[i], out.at[block], sems.at[i])
        copy.start()
        copies.append(copy)
    for copy in copies:
        copy.wait()


def update_part(moves, dirs, basis_t, out):
    n = len(moves)
    rows, rank = dirs[0].shape
    cols = basis_t.shape[1]
    aliased = 0 if out is None else 1
    args = (*dirs, basis_t) + ((out,) if aliased else ())
    return call(
        functools.partial(update_body, moves, aliased),
        [((NX * NH, rows, cols), bf16)],
        len(args),
        scratch=[pltpu.VMEM((n, rows, cols), bf16), pltpu.SemaphoreType.DMA((n,))],
        in_specs=[VMEM] * (n + 1) + [ANY] * aliased,
        out_specs=[ANY],
        input_output_aliases={n + 1: 0} if aliased else {},
    )(*args)[0]


def per_device(features, out_grads, proj_basis, first_moment, second_moment):
    tokens, _ = features.shape
    width, rank = proj_basis.shape
    rows = first_moment.shape[1]
    toks = tokens // NX

    own, s1, s2, s3 = call(
        project_body, [((toks, rank), f32)] + [((toks, rank), bf16)] * 3, 2
    )(features, proj_basis)
    r2, r1, r3 = to_x(s2, 2), to_x(s1, 1), to_x(s3, 3)

    block = (NY, NZ, rows, tokens)
    keep, send, basis_t = call(
        turn_body,
        [(block, bf16), (block, bf16), ((rank, width), bf16)],
        2,
        scratch=[pltpu.VMEM((NZ * NC * rows, tokens), bf16)],
    )(out_grads, proj_basis)
    other = to_core(send)

    total, sent = call(sum_x_body, [((toks, rank), f32), ((toks, rank), bf16)], 4)(own, r1, r2, r3)
    p0 = call(sum_h_body, [((toks, rank), bf16)], 2)(total, to_h(sent))[0]
    p2, p1, p3 = to_x(p0, 2), to_x(p0, 1), to_x(p0, 3)
    q = to_core(jnp.concatenate([p0, p1, p2, p3], axis=0))

    own, s1, s2, s3 = call(
        low_body, [((NZ * rows, rank), f32)] + [((NZ * rows, rank), bf16)] * 3, 7
    )(keep, other, p0, p1, p2, p3, q)
    r2, r1, r3 = to_y(s2, 2), to_y(s1, 1), to_y(s3, 3)
    own, s1, s2, s3 = call(
        sum_y_body, [((rows, rank), f32)] + [((rows, rank), bf16)] * 3, 4
    )(own, r1, r2, r3)
    r3, r2, r1 = to_z(s3, 3), to_z(s2, 2), to_z(s1, 1)
    first_new, second_new, d0 = call(
        adam_body, [((1, rows, rank), f32)] * 2 + [((rows, rank), bf16)], 6
    )(own, r1, r2, r3, first_moment, second_moment)

    e0 = to_h(d0)
    d2, d1, d3 = to_x(d0, 2), to_x(d0, 1), to_x(d0, 3)
    e2, e1, e3 = to_x(e0, 2), to_x(e0, 1), to_x(e0, 3)
    update = update_part([(0, 0)], [d0], basis_t, None)
    update = update_part([(1, 0), (2, 0), (3, 0), (0, 1)], [d1, d2, d3, e0], basis_t, update)
    update = update_part([(1, 1), (2, 1), (3, 1)], [e1, e2, e3], basis_t, update)
    return (update, first_new, second_new)


def solution(mesh):
    return jax.shard_map(
        per_device,
        mesh=mesh,
        in_specs=(
            P("dp", "shard"),
            P("dp", "shard"),
            P("shard", None),
            P("shard", "dp", None),
            P("shard", "dp", None),
        ),
        out_specs=(P(None, "dp", "shard"), P("shard", "dp", None), P("shard", "dp", None)),
        check_vma=False,
    )
```

```python
import functools

import jax
import jax.numpy as jnp
from jax import lax
from jax.experimental import pallas as pl
from jax.experimental.pallas import tpu as pltpu
from jax.sharding import PartitionSpec as P

beta_first = 0.9
beta_second = 0.99
correct_first = 0.9999734386011124
correct_second = 0.6339676587267705
epsilon = 1e-08
galore_scale = 4.0

bf16, f32 = jnp.bfloat16, jnp.float32
NY, NZ, NC, NX, NH = 4, 4, 2, 4, 2
VMEM = pl.BlockSpec(memory_space=pltpu.VMEM)
ANY = pl.BlockSpec(memory_space=pl.ANY)
HBM = pl.BlockSpec(memory_space=pltpu.HBM)


def dp_perm(step):
    pairs = []
    for y in range(NY):
        for z in range(NZ):
            for c in range(NC):
                ty, tz, tc = step(y, z, c)
                pairs.append(((y * NZ + z) * NC + c, ((ty % NY) * NZ + tz) * NC + tc))
    return pairs


def shard_perm(step):
    pairs = []
    for x in range(NX):
        for h in range(NH):
            tx, th = step(x, h)
            pairs.append((x * NH + h, (tx % NX) * NH + th))
    return pairs


def to_core(a):
    return lax.ppermute(a, "dp", dp_perm(lambda y, z, c: (y, z, 1 - c)))


def to_y(a, k):
    return lax.ppermute(a, "dp", dp_perm(lambda y, z, c: (y + k, z, c)))


def to_z(a, k):
    return lax.ppermute(a, "dp", dp_perm(lambda y, z, c: (y, z ^ k, c)))


def to_x(a, k):
    return lax.ppermute(a, "shard", shard_perm(lambda x, h: (x + k, h)))


def to_h(a):
    return lax.ppermute(a, "shard", shard_perm(lambda x, h: (x, 1 - h)))


def place():
    dp, shard = lax.axis_index("dp"), lax.axis_index("shard")
    return dp // (NZ * NC), (dp // NC) % NZ, dp % NC, shard // NH, shard % NH


def call(body, outs, n_in, scratch=(), limit=16, **kw):
    return pl.pallas_call(
        body,
        out_shape=[jax.ShapeDtypeStruct(s, d) for s, d in outs],
        in_specs=kw.pop("in_specs", [VMEM] * n_in),
        out_specs=kw.pop("out_specs", [VMEM] * len(outs)),
        scratch_shapes=list(scratch),
        compiler_params=pltpu.CompilerParams(vmem_limit_bytes=limit << 20),
        **kw,
    )


def project_body(feat, basis, own, s1, s2, s3, fbuf, bbuf, sems):
    _, _, _, x, _ = place()
    rows = own.shape[0]
    order = ((2, s2), (1, s1), (3, s3), (0, own))
    copies = [pltpu.make_async_copy(basis, bbuf, sems.at[NX])]
    for k, _ in order:
        start = pl.multiple_of(lax.rem(x + k, NX) * rows, rows)
        copies.append(pltpu.make_async_copy(feat.at[pl.ds(start, rows), :], fbuf.at[k], sems.at[k]))
    for copy in copies:
        copy.start()
    copies[0].wait()
    for (k, out), copy in zip(order, copies[1:]):
        copy.wait()
        part = jnp.dot(fbuf[k], bbuf[...], preferred_element_type=f32)
        out[...] = part.astype(out.dtype)


def turn_body(grads, basis, _, keep, send, basis_t, gbuf, bbuf, tmp, sems):
    y, z, c, x, _ = place()
    rows = keep.shape[2]
    wide = NZ * NC * rows
    toks = gbuf.shape[1] // NX
    copies = []
    for ry in range(NY):
        col = pl.multiple_of(lax.rem(y + ry, NY) * wide, 128)
        copies.append(pltpu.make_async_copy(grads.at[:, pl.ds(col, wide)], gbuf.at[ry], sems.at[ry]))
    copies.append(pltpu.make_async_copy(basis, bbuf, sems.at[NY]))
    for copy in copies:
        copy.start()
    for ry in range(NY):
        copies[ry].wait()
        for k in range(NX):
            tok = pl.multiple_of(lax.rem(x + NX - k, NX) * toks, toks)
            tmp[:, k * toks : (k + 1) * toks] = gbuf[ry, pl.ds(tok, toks), :].T
        for rz in range(NZ):
            for cc, out in ((0, keep), (1, send)):
                start = pl.multiple_of(((z ^ rz) * NC + (c ^ cc)) * rows, 16)
                out[ry, rz] = tmp[pl.ds(start, rows), :]
    copies[NY].wait()
    basis_t[...] = bbuf[...].T


def sum_x_body(own, r1, r2, r3, total, sent):
    t = own[...] + r1[...].astype(f32) + r2[...].astype(f32) + r3[...].astype(f32)
    total[...] = t
    sent[...] = t.astype(bf16)


def sum_h_body(own, other, out):
    out[...] = (own[...] + other[...].astype(f32)).astype(bf16)


def low_own_body(keep, p0, p1, p2, p3, acc):
    rows, toks = keep.shape[1] * keep.shape[2], keep.shape[3]
    proj = jnp.concatenate([p[...] for p in (p0, p1, p2, p3)], axis=0)
    for ry in range(NY):
        a = keep[ry].reshape(rows, toks)
        acc[ry] = jnp.dot(a, proj, preferred_element_type=f32)


def low_body(group, acc, other, q, *refs):
    outs = refs[-NY:]
    rows, toks = other.shape[1] * other.shape[2], other.shape[3]
    half = rows // 2
    for ry in (2, 1, 3, 0):
        part = other[ry, group * NZ // 2 : (group + 1) * NZ // 2].reshape(half, toks)
        t = acc[ry, group * half : (group + 1) * half, :]
        t = t + jnp.dot(part, q[...], preferred_element_type=f32)
        outs[ry][...] = t.astype(outs[ry].dtype)


def sum_y_body(own, r1, r2, r3, first, second):
    rows = first.shape[0]
    for i, out in enumerate((first, second)):
        part = slice(i * rows, (i + 1) * rows)
        t = own[part, :] + r1[part, :].astype(f32) + r2[part, :].astype(f32) + r3[part, :].astype(f32)
        out[...] = t.astype(out.dtype)


def adam_body(own, r1, r2, r3, first, second, first_new, second_new, direction):
    g = own[...] + r1[...].astype(f32) + r2[...].astype(f32) + r3[...].astype(f32)
    m = beta_first * first[0] + (1.0 - beta_first) * g
    v = beta_second * second[0] + (1.0 - beta_second) * g * g
    first_new[0] = m
    second_new[0] = v
    d = m / correct_first / (jnp.sqrt(v / correct_second) + epsilon)
    direction[...] = d.astype(bf16)


def update_body(moves, aliased, *refs):
    n = len(moves)
    dirs, basis_t = refs[:n], refs[n]
    out, buf, sems = refs[n + 1 + aliased :]
    _, _, _, x, h = place()
    copies = []
    for i, (k, flip) in enumerate(moves):
        t = galore_scale * jnp.dot(dirs[i][...], basis_t[...], preferred_element_type=f32)
        buf[i] = t.astype(bf16)
        block = lax.rem(x + NX - k, NX) * NH + (h ^ flip)
        copy = pltpu.make_async_copy(buf.at[i], out.at[block], sems.at[i])
        copy.start()
        copies.append(copy)
    for copy in copies:
        copy.wait()


def update_part(moves, dirs, basis_t, out):
    n = len(moves)
    rows, rank = dirs[0].shape
    cols = basis_t.shape[1]
    aliased = 0 if out is None else 1
    args = (*dirs, basis_t) + ((out,) if aliased else ())
    return call(
        functools.partial(update_body, moves, aliased),
        [((NX * NH, rows, cols), bf16)],
        len(args),
        scratch=[pltpu.VMEM((n, rows, cols), bf16), pltpu.SemaphoreType.DMA((n,))],
        in_specs=[VMEM] * (n + 1) + [ANY] * aliased,
        out_specs=[ANY],
        input_output_aliases={n + 1: 0} if aliased else {},
    )(*args)[0]


def per_device(features, out_grads, proj_basis, first_moment, second_moment):
    tokens, _ = features.shape
    width, rank = proj_basis.shape
    rows = first_moment.shape[1]
    toks = tokens // NX

    features = pltpu.with_memory_space_constraint(features, pltpu.HBM)
    basis_in = pltpu.with_memory_space_constraint(proj_basis, pltpu.HBM)
    own, s1, s2, s3 = call(
        project_body,
        [((toks, rank), f32)] + [((toks, rank), bf16)] * 3,
        2,
        scratch=[
            pltpu.VMEM((NX, toks, width), bf16),
            pltpu.VMEM((width, rank), bf16),
            pltpu.SemaphoreType.DMA((NX + 1,)),
        ],
        in_specs=[HBM] * 2,
        limit=16,
    )(features, basis_in)
    r2, r1, r3 = to_x(s2, 2), to_x(s1, 1), to_x(s3, 3)

    block = (NY, NZ, rows, tokens)
    wide = NZ * NC * rows
    keep, send, basis_t = call(
        turn_body,
        [(block, bf16), (block, bf16), ((rank, width), bf16)],
        3,
        scratch=[
            pltpu.VMEM((NY, tokens, wide), bf16),
            pltpu.VMEM((width, rank), bf16),
            pltpu.VMEM((wide, tokens), bf16),
            pltpu.SemaphoreType.DMA((NY + 1,)),
        ],
        in_specs=[HBM, HBM, ANY],
    )(out_grads, proj_basis, own)
    total, sent = call(sum_x_body, [((toks, rank), f32), ((toks, rank), bf16)], 4)(own, r1, r2, r3)
    send, sent = lax.optimization_barrier((send, sent))
    other = to_core(send)
    p0 = call(sum_h_body, [((toks, rank), bf16)], 2)(total, to_h(sent))[0]
    p2, p1, p3 = to_x(p0, 2), to_x(p0, 1), to_x(p0, 3)
    q = to_core(jnp.concatenate([p0, p1, p2, p3], axis=0))

    acc = call(low_own_body, [((NY, NZ * rows, rank), f32)], 5)(keep, p0, p1, p2, p3)[0]
    half = (NZ // 2 * rows, rank)
    sums = [(half, f32)] + [(half, bf16)] * 3
    own_b, b1, b2, b3 = call(functools.partial(low_body, 1), sums, 3)(acc, other, q)
    b2, b1, b3 = to_y(b2, 2), to_y(b1, 1), to_y(b3, 3)
    own_a, a1, a2, a3 = call(
        functools.partial(low_body, 0), sums, 4, in_specs=[VMEM] * 3 + [ANY]
    )(acc, other, q, b1)
    a2, a1, a3 = to_y(a2, 2), to_y(a1, 1), to_y(a3, 3)
    s2, s3 = call(sum_y_body, [((rows, rank), bf16)] * 2, 4)(own_b, b1, b2, b3)
    r3, r2 = to_z(s3, 3), to_z(s2, 2)
    own, s1 = call(sum_y_body, [((rows, rank), f32), ((rows, rank), bf16)], 4)(own_a, a1, a2, a3)
    r1 = to_z(s1, 1)
    first_new, second_new, d0 = call(
        adam_body, [((1, rows, rank), f32)] * 2 + [((rows, rank), bf16)], 6
    )(own, r1, r2, r3, first_moment, second_moment)

    e0 = to_h(d0)
    d2, d1, d3 = to_x(d0, 2), to_x(d0, 1), to_x(d0, 3)
    e2, e1, e3 = to_x(e0, 2), to_x(e0, 1), to_x(e0, 3)
    update = update_part([(0, 0)], [d0], basis_t, None)
    update = update_part([(1, 0), (2, 0), (3, 0), (0, 1)], [d1, d2, d3, e0], basis_t, update)
    update = update_part([(1, 1), (2, 1), (3, 1)], [e1, e2, e3], basis_t, update)
    return (update, first_new, second_new)


def solution(mesh):
    return jax.shard_map(
        per_device,
        mesh=mesh,
        in_specs=(
            P("dp", "shard"),
            P("dp", "shard"),
            P("shard", None),
            P("shard", "dp", None),
            P("shard", "dp", None),
        ),
        out_specs=(P(None, "dp", "shard"), P("shard", "dp", None), P("shard", "dp", None)),
        check_vma=False,
    )
```

```python
import functools

import jax
import jax.numpy as jnp
from jax import lax
from jax.experimental import pallas as pl
from jax.experimental.pallas import tpu as pltpu
from jax.sharding import PartitionSpec as P

beta_first = 0.9
beta_second = 0.99
correct_first = 0.9999734386011124
correct_second = 0.6339676587267705
epsilon = 1e-08
galore_scale = 4.0

bf16, f32 = jnp.bfloat16, jnp.float32
NY, NZ, NC, NX, NH = 4, 4, 2, 4, 2
SPLIT = 2
VMEM = pl.BlockSpec(memory_space=pltpu.VMEM)
ANY = pl.BlockSpec(memory_space=pl.ANY)
HBM = pl.BlockSpec(memory_space=pltpu.HBM)


def dp_perm(step):
    pairs = []
    for y in range(NY):
        for z in range(NZ):
            for c in range(NC):
                ty, tz, tc = step(y, z, c)
                pairs.append(((y * NZ + z) * NC + c, ((ty % NY) * NZ + tz) * NC + tc))
    return pairs


def shard_perm(step):
    pairs = []
    for x in range(NX):
        for h in range(NH):
            tx, th = step(x, h)
            pairs.append((x * NH + h, (tx % NX) * NH + th))
    return pairs


def to_core(a):
    return lax.ppermute(a, "dp", dp_perm(lambda y, z, c: (y, z, 1 - c)))


def to_y(a, k):
    return lax.ppermute(a, "dp", dp_perm(lambda y, z, c: (y + k, z, c)))


def to_z(a, k):
    return lax.ppermute(a, "dp", dp_perm(lambda y, z, c: (y, z ^ k, c)))


def to_x(a, k):
    return lax.ppermute(a, "shard", shard_perm(lambda x, h: (x + k, h)))


def to_h(a):
    return lax.ppermute(a, "shard", shard_perm(lambda x, h: (x, 1 - h)))


def place():
    dp, shard = lax.axis_index("dp"), lax.axis_index("shard")
    return dp // (NZ * NC), (dp // NC) % NZ, dp % NC, shard // NH, shard % NH


def call(body, outs, n_in, scratch=(), limit=16, **kw):
    return pl.pallas_call(
        body,
        out_shape=[jax.ShapeDtypeStruct(s, d) for s, d in outs],
        in_specs=kw.pop("in_specs", [VMEM] * n_in),
        out_specs=kw.pop("out_specs", [VMEM] * len(outs)),
        scratch_shapes=list(scratch),
        compiler_params=pltpu.CompilerParams(vmem_limit_bytes=limit << 20),
        **kw,
    )


def project_body(feat, basis, own, s1, s2, s3, fbuf, bbuf, sems):
    _, _, _, x, _ = place()
    rows = own.shape[0]
    order = ((2, s2), (1, s1), (3, s3), (0, own))
    part = basis.shape[0] // NX
    copies = []
    for i in range(NX):
        cut = pl.ds(i * part, part)
        copies.append(pltpu.make_async_copy(basis.at[cut, :], bbuf.at[cut, :], sems.at[NX + i]))
    for k, _ in order:
        start = pl.multiple_of(lax.rem(x + k, NX) * rows, rows)
        copies.append(pltpu.make_async_copy(feat.at[pl.ds(start, rows), :], fbuf.at[k], sems.at[k]))
    for copy in copies:
        copy.start()
    for copy in copies[:NX]:
        copy.wait()
    for (k, out), copy in zip(order, copies[NX:]):
        copy.wait()
        t = jnp.dot(fbuf[k], bbuf[...], preferred_element_type=f32)
        out[...] = t.astype(out.dtype)


def turn_body(grads, basis, _, keep, *refs):
    sends = refs[:SPLIT]
    basis_t, gbuf, bbuf, tmp, sems = refs[SPLIT:]
    y, z, c, x, _ = place()
    rows = keep.shape[2]
    wide = NZ * NC * rows
    toks = gbuf.shape[1] // NX
    copies = []
    for ry in range(NY):
        col = pl.multiple_of(lax.rem(y + ry, NY) * wide, 128)
        copies.append(pltpu.make_async_copy(grads.at[:, pl.ds(col, wide)], gbuf.at[ry], sems.at[ry]))
    copies.append(pltpu.make_async_copy(basis, bbuf, sems.at[NY]))
    for copy in copies:
        copy.start()
    for ry in range(NY):
        copies[ry].wait()
        for k in range(NX):
            tok = pl.multiple_of(lax.rem(x + NX - k, NX) * toks, toks)
            tmp[:, k * toks : (k + 1) * toks] = gbuf[ry, pl.ds(tok, toks), :].T
        for rz in range(NZ):
            base = (z ^ rz) * NC
            keep[ry, rz] = tmp[pl.ds(pl.multiple_of((base + c) * rows, 16), rows), :]
            other = tmp[pl.ds(pl.multiple_of((base + 1 - c) * rows, 16), rows), :]
            sends[ry * SPLIT // NY][ry % (NY // SPLIT), rz] = other
    copies[NY].wait()
    basis_t[...] = bbuf[...].T


def sum_x_body(own, r1, r2, r3, total, sent):
    t = own[...] + r1[...].astype(f32) + r2[...].astype(f32) + r3[...].astype(f32)
    total[...] = t
    sent[...] = t.astype(bf16)


def sum_h_body(own, other, out):
    out[...] = (own[...] + other[...].astype(f32)).astype(bf16)


def low_own_body(keep, p0, p1, p2, p3, acc):
    rows, toks = keep.shape[1] * keep.shape[2], keep.shape[3]
    proj = jnp.concatenate([p[...] for p in (p0, p1, p2, p3)], axis=0)
    for ry in range(NY):
        a = keep[ry].reshape(rows, toks)
        acc[ry] = jnp.dot(a, proj, preferred_element_type=f32)


def low_far_body(rz, acc, q, *refs):
    other, outs = refs[:SPLIT], refs[SPLIT:]
    rows = other[0].shape[2]
    for ry in (2, 1, 3, 0):
        t = acc[ry, rz * rows : (rz + 1) * rows, :]
        t = t + jnp.dot(other[ry * SPLIT // NY][ry % (NY // SPLIT), rz], q[...], preferred_element_type=f32)
        outs[ry][...] = t.astype(outs[ry].dtype)


def low_near_body(acc, q, *refs):
    other, (own, send) = refs[:SPLIT], refs[SPLIT:]
    rows = other[0].shape[2]
    for ry in range(NY):
        for rz, out in ((1, send), (0, own)):
            t = acc[ry, rz * rows : (rz + 1) * rows, :]
            t = t + jnp.dot(other[ry * SPLIT // NY][ry % (NY // SPLIT), rz], q[...], preferred_element_type=f32)
            out[ry * rows : (ry + 1) * rows, :] = t.astype(out.dtype)


def sum_far_body(own, r1, r2, r3, out):
    t = own[...] + r1[...].astype(f32) + r2[...].astype(f32) + r3[...].astype(f32)
    out[...] = t.astype(out.dtype)


def sum_near_body(own, near, total, s1, s2, s3):
    rows = total.shape[0]
    for ry, out in ((2, s2), (1, s1), (3, s3), (0, total)):
        part = slice(ry * rows, (ry + 1) * rows)
        out[...] = (own[part, :] + near[part, :].astype(f32)).astype(out.dtype)


def direction_body(z3, z2, own, y1, y2, y3, first, second, grad, direction):
    g = own[...] + y1[...].astype(f32) + y2[...].astype(f32) + y3[...].astype(f32)
    g = g + z2[...].astype(f32) + z3[...].astype(f32)
    grad[...] = g
    m = beta_first * first[0] + (1.0 - beta_first) * g
    v = beta_second * second[0] + (1.0 - beta_second) * g * g
    d = m / correct_first / (jnp.sqrt(v / correct_second) + epsilon)
    direction[...] = d.astype(bf16)


def moments_body(grad, first, second, first_new, second_new):
    g = grad[...]
    first_new[0] = beta_first * first[0] + (1.0 - beta_first) * g
    second_new[0] = beta_second * second[0] + (1.0 - beta_second) * g * g


def update_body(moves, aliased, *refs):
    n = len(moves)
    dirs, basis_t = refs[:n], refs[n]
    out, buf, sems = refs[n + 1 + aliased :]
    _, _, _, x, h = place()
    copies = []
    for i, (k, flip) in enumerate(moves):
        t = galore_scale * jnp.dot(dirs[i][...], basis_t[...], preferred_element_type=f32)
        buf[i] = t.astype(bf16)
        block = lax.rem(x + NX - k, NX) * NH + (h ^ flip)
        copy = pltpu.make_async_copy(buf.at[i], out.at[block], sems.at[i])
        copy.start()
        copies.append(copy)
    for copy in copies:
        copy.wait()


def update_part(moves, dirs, basis_t, out):
    n = len(moves)
    rows, rank = dirs[0].shape
    cols = basis_t.shape[1]
    aliased = 0 if out is None else 1
    args = (*dirs, basis_t) + ((out,) if aliased else ())
    return call(
        functools.partial(update_body, moves, aliased),
        [((NX * NH, rows, cols), bf16)],
        len(args),
        scratch=[pltpu.VMEM((n, rows, cols), bf16), pltpu.SemaphoreType.DMA((n,))],
        in_specs=[VMEM] * (n + 1) + [ANY] * aliased,
        out_specs=[ANY],
        input_output_aliases={n + 1: 0} if aliased else {},
    )(*args)[0]


def per_device(features, out_grads, proj_basis, first_moment, second_moment):
    tokens, _ = features.shape
    width, rank = proj_basis.shape
    rows = first_moment.shape[1]
    toks = tokens // NX

    features = pltpu.with_memory_space_constraint(features, pltpu.HBM)
    grads_in = pltpu.with_memory_space_constraint(out_grads, pltpu.HBM)
    basis_in = pltpu.with_memory_space_constraint(proj_basis, pltpu.HBM)
    own, s1, s2, s3 = call(
        project_body,
        [((toks, rank), f32)] + [((toks, rank), bf16)] * 3,
        2,
        scratch=[
            pltpu.VMEM((NX, toks, width), bf16),
            pltpu.VMEM((width, rank), bf16),
            pltpu.SemaphoreType.DMA((2 * NX,)),
        ],
        in_specs=[HBM] * 2,
        limit=16,
    )(features, basis_in)
    r2, r1, r3 = to_x(s2, 2), to_x(s1, 1), to_x(s3, 3)

    block = (NY, NZ, rows, tokens)
    wide = NZ * NC * rows
    keep, *sends, basis_t = call(
        turn_body,
        [(block, bf16)] + [((NY // SPLIT, NZ, rows, tokens), bf16)] * SPLIT + [((rank, width), bf16)],
        3,
        scratch=[
            pltpu.VMEM((NY, tokens, wide), bf16),
            pltpu.VMEM((width, rank), bf16),
            pltpu.VMEM((wide, tokens), bf16),
            pltpu.SemaphoreType.DMA((NY + 1,)),
        ],
        in_specs=[HBM, HBM, ANY],
    )(grads_in, basis_in, own)
    total, sent = call(sum_x_body, [((toks, rank), f32), ((toks, rank), bf16)], 4)(own, r1, r2, r3)
    half_sum = to_h(sent)
    other = [to_core(a) for a in sends]
    p0 = call(sum_h_body, [((toks, rank), bf16)], 2)(total, half_sum)[0]
    p2, p1, p3 = to_x(p0, 2), to_x(p0, 1), to_x(p0, 3)
    q = to_core(jnp.concatenate([p0, p1, p2, p3], axis=0))

    acc = call(low_own_body, [((NY, NZ * rows, rank), f32)], 5)(keep, p0, p1, p2, p3)[0]
    one, four = (rows, rank), (NY * rows, rank)

    def low_far(rz):
        return call(functools.partial(low_far_body, rz), [(one, f32)] + [(one, bf16)] * 3, 2 + SPLIT)(
            acc, q, *other
        )

    def over_y(s1, s2, s3):
        r2, r1, r3 = to_y(s2, 2), to_y(s1, 1), to_y(s3, 3)
        return r1, r2, r3

    own3, *far3 = low_far(3)
    far3 = over_y(*far3)
    near, send = call(low_near_body, [(four, f32), (four, bf16)], 2 + SPLIT)(acc, q, *other)
    send = to_z(send, 1)
    own2, *far2 = low_far(2)
    far2 = over_y(*far2)
    z3 = to_z(call(sum_far_body, [(one, bf16)], 4)(own3, *far3)[0], 3)
    z2 = to_z(call(sum_far_body, [(one, bf16)], 4)(own2, *far2)[0], 2)
    own, y1, y2, y3 = call(sum_near_body, [(one, f32)] + [(one, bf16)] * 3, 2)(near, send)
    y1, y2, y3 = over_y(y1, y2, y3)
    grad, d0 = call(direction_body, [(one, f32), (one, bf16)], 8)(
        z3, z2, own, y1, y2, y3, first_moment, second_moment
    )
    e0 = to_h(d0)
    d2, d1, d3 = to_x(d0, 2), to_x(d0, 1), to_x(d0, 3)
    update = update_part([(0, 0)], [d0], basis_t, None)
    e0, update = lax.optimization_barrier((e0, update))
    e2, e1, e3 = to_x(e0, 2), to_x(e0, 1), to_x(e0, 3)
    grad, _ = lax.optimization_barrier((grad, e0))
    first_new, second_new = call(moments_body, [((1, rows, rank), f32)] * 2, 3)(
        grad, first_moment, second_moment
    )
    update = update_part([(1, 0), (2, 0), (3, 0), (0, 1)], [d1, d2, d3, e0], basis_t, update)
    update = update_part([(1, 1), (2, 1), (3, 1)], [e1, e2, e3], basis_t, update)
    return (update, first_new, second_new)


def solution(mesh):
    return jax.shard_map(
        per_device,
        mesh=mesh,
        in_specs=(
            P("dp", "shard"),
            P("dp", "shard"),
            P("shard", None),
            P("shard", "dp", None),
            P("shard", "dp", None),
        ),
        out_specs=(P(None, "dp", "shard"), P("shard", "dp", None), P("shard", "dp", None)),
        check_vma=False,
    )
```

```python
import functools

import jax
import jax.numpy as jnp
from jax import lax
from jax.experimental import pallas as pl
from jax.experimental.pallas import tpu as pltpu
from jax.sharding import PartitionSpec as P

beta_first = 0.9
beta_second = 0.99
correct_first = 0.9999734386011124
correct_second = 0.6339676587267705
epsilon = 1e-08
galore_scale = 4.0

bf16, f32 = jnp.bfloat16, jnp.float32
NY, NZ, NC, NX, NH = 4, 4, 2, 4, 2
SPLIT = 2
VMEM = pl.BlockSpec(memory_space=pltpu.VMEM)
ANY = pl.BlockSpec(memory_space=pl.ANY)
HBM = pl.BlockSpec(memory_space=pltpu.HBM)


def dp_perm(step):
    pairs = []
    for y in range(NY):
        for z in range(NZ):
            for c in range(NC):
                ty, tz, tc = step(y, z, c)
                pairs.append(((y * NZ + z) * NC + c, ((ty % NY) * NZ + tz) * NC + tc))
    return pairs


def shard_perm(step):
    pairs = []
    for x in range(NX):
        for h in range(NH):
            tx, th = step(x, h)
            pairs.append((x * NH + h, (tx % NX) * NH + th))
    return pairs


def to_core(a):
    return lax.ppermute(a, "dp", dp_perm(lambda y, z, c: (y, z, 1 - c)))


def to_y(a, k):
    return lax.ppermute(a, "dp", dp_perm(lambda y, z, c: (y + k, z, c)))


def to_z(a, k):
    return lax.ppermute(a, "dp", dp_perm(lambda y, z, c: (y, z ^ k, c)))


def to_x(a, k):
    return lax.ppermute(a, "shard", shard_perm(lambda x, h: (x + k, h)))


def to_h(a):
    return lax.ppermute(a, "shard", shard_perm(lambda x, h: (x, 1 - h)))


def place():
    dp, shard = lax.axis_index("dp"), lax.axis_index("shard")
    return dp // (NZ * NC), (dp // NC) % NZ, dp % NC, shard // NH, shard % NH


def call(body, outs, n_in, scratch=(), limit=16, **kw):
    return pl.pallas_call(
        body,
        out_shape=[jax.ShapeDtypeStruct(s, d) for s, d in outs],
        in_specs=kw.pop("in_specs", [VMEM] * n_in),
        out_specs=kw.pop("out_specs", [VMEM] * len(outs)),
        scratch_shapes=list(scratch),
        compiler_params=pltpu.CompilerParams(vmem_limit_bytes=limit << 20),
        **kw,
    )


def project_body(feat, basis, own, s1, s2, s3, fbuf, bbuf, acc, sems):
    _, _, _, x, _ = place()
    rows = own.shape[0]
    part = basis.shape[0] // NX
    copies = []
    for i in range(NX):
        cut = pl.ds(i * part, part)
        copies.append(pltpu.make_async_copy(basis.at[cut, :], bbuf.at[cut, :], sems.at[NX + i]))
        copies.append(pltpu.make_async_copy(feat.at[:, cut], fbuf.at[i], sems.at[i]))
    for copy in copies:
        copy.start()
    for i in range(NX):
        copies[2 * i].wait()
        copies[2 * i + 1].wait()
        t = jnp.dot(fbuf[i], bbuf[i * part : (i + 1) * part, :], preferred_element_type=f32)
        acc[...] = t if i == 0 else acc[...] + t
    for k, out in ((1, s1), (3, s3), (2, s2), (0, own)):
        start = pl.multiple_of(lax.rem(x + k, NX) * rows, rows)
        out[...] = acc[pl.ds(start, rows), :].astype(out.dtype)


def turn_body(grads, basis, _, keep, *refs):
    sends = refs[:SPLIT]
    basis_t, gbuf, bbuf, tmp, sems = refs[SPLIT:]
    y, z, c, x, _ = place()
    rows = keep.shape[2]
    wide = NZ * NC * rows
    toks = gbuf.shape[1] // NX
    copies = []
    for ry in range(NY):
        col = pl.multiple_of(lax.rem(y + ry, NY) * wide, 128)
        copies.append(pltpu.make_async_copy(grads.at[:, pl.ds(col, wide)], gbuf.at[ry], sems.at[ry]))
    copies.append(pltpu.make_async_copy(basis, bbuf, sems.at[NY]))
    for copy in copies:
        copy.start()
    for ry in range(NY):
        copies[ry].wait()
        for k in range(NX):
            tok = pl.multiple_of(lax.rem(x + NX - k, NX) * toks, toks)
            tmp[:, k * toks : (k + 1) * toks] = gbuf[ry, pl.ds(tok, toks), :].T
        for rz in range(NZ):
            base = (z ^ rz) * NC
            keep[ry, rz] = tmp[pl.ds(pl.multiple_of((base + c) * rows, 16), rows), :]
            other = tmp[pl.ds(pl.multiple_of((base + 1 - c) * rows, 16), rows), :]
            sends[ry * SPLIT // NY][ry % (NY // SPLIT), rz] = other
    copies[NY].wait()
    basis_t[...] = bbuf[...].T


def sum_x_body(own, r1, r2, r3, total, sent):
    t = own[...] + r1[...].astype(f32) + r2[...].astype(f32) + r3[...].astype(f32)
    total[...] = t
    sent[...] = t.astype(bf16)


def sum_h_body(own, other, out):
    out[...] = (own[...] + other[...].astype(f32)).astype(bf16)


def low_own_body(keep, p0, p1, p2, p3, acc):
    rows, toks = keep.shape[1] * keep.shape[2], keep.shape[3]
    proj = jnp.concatenate([p[...] for p in (p0, p1, p2, p3)], axis=0)
    for ry in range(NY):
        a = keep[ry].reshape(rows, toks)
        acc[ry] = jnp.dot(a, proj, preferred_element_type=f32)


def low_far_body(rz, acc, q, *refs):
    other, outs = refs[:SPLIT], refs[SPLIT:]
    rows = other[0].shape[2]
    for ry in (2, 1, 3, 0):
        t = acc[ry, rz * rows : (rz + 1) * rows, :]
        t = t + jnp.dot(other[ry * SPLIT // NY][ry % (NY // SPLIT), rz], q[...], preferred_element_type=f32)
        outs[ry][...] = t.astype(outs[ry].dtype)


def low_near_body(rz, acc, q, *refs):
    other, out = refs[:SPLIT], refs[SPLIT]
    rows = other[0].shape[2]
    for ry in range(NY):
        t = acc[ry, rz * rows : (rz + 1) * rows, :]
        t = t + jnp.dot(other[ry * SPLIT // NY][ry % (NY // SPLIT), rz], q[...], preferred_element_type=f32)
        out[ry * rows : (ry + 1) * rows, :] = t.astype(out.dtype)


def sum_far_body(own, r1, r2, r3, out):
    t = own[...] + r1[...].astype(f32) + r2[...].astype(f32) + r3[...].astype(f32)
    out[...] = t.astype(out.dtype)


def sum_near_body(own, near, total, s1, s2, s3):
    rows = total.shape[0]
    for ry, out in ((2, s2), (1, s1), (3, s3), (0, total)):
        part = slice(ry * rows, (ry + 1) * rows)
        out[...] = (own[part, :] + near[part, :].astype(f32)).astype(out.dtype)


def direction_body(z3, z2, own, y1, y2, y3, first, second, grad, direction):
    g = own[...] + y1[...].astype(f32) + y2[...].astype(f32) + y3[...].astype(f32)
    g = g + z2[...].astype(f32) + z3[...].astype(f32)
    grad[...] = g
    m = beta_first * first[0] + (1.0 - beta_first) * g
    v = beta_second * second[0] + (1.0 - beta_second) * g * g
    d = m / correct_first / (jnp.sqrt(v / correct_second) + epsilon)
    direction[...] = d.astype(bf16)


def moments_body(grad, first, second, first_new, second_new):
    g = grad[...]
    first_new[0] = beta_first * first[0] + (1.0 - beta_first) * g
    second_new[0] = beta_second * second[0] + (1.0 - beta_second) * g * g


def update_body(moves, aliased, *refs):
    n = len(moves)
    dirs, basis_t = refs[:n], refs[n]
    out, buf, sems = refs[n + 1 + aliased :]
    _, _, _, x, h = place()
    copies = []
    for i, (k, flip) in enumerate(moves):
        t = galore_scale * jnp.dot(dirs[i][...], basis_t[...], preferred_element_type=f32)
        buf[i] = t.astype(bf16)
        block = lax.rem(x + NX - k, NX) * NH + (h ^ flip)
        copy = pltpu.make_async_copy(buf.at[i], out.at[block], sems.at[i])
        copy.start()
        copies.append(copy)
    for copy in copies:
        copy.wait()


def update_part(moves, dirs, basis_t, out):
    n = len(moves)
    rows, rank = dirs[0].shape
    cols = basis_t.shape[1]
    aliased = 0 if out is None else 1
    args = (*dirs, basis_t) + ((out,) if aliased else ())
    return call(
        functools.partial(update_body, moves, aliased),
        [((NX * NH, rows, cols), bf16)],
        len(args),
        scratch=[pltpu.VMEM((n, rows, cols), bf16), pltpu.SemaphoreType.DMA((n,))],
        in_specs=[VMEM] * (n + 1) + [ANY] * aliased,
        out_specs=[ANY],
        input_output_aliases={n + 1: 0} if aliased else {},
    )(*args)[0]


def per_device(features, out_grads, proj_basis, first_moment, second_moment):
    tokens, _ = features.shape
    width, rank = proj_basis.shape
    rows = first_moment.shape[1]
    toks = tokens // NX

    features = pltpu.with_memory_space_constraint(features, pltpu.HBM)
    grads_in = pltpu.with_memory_space_constraint(out_grads, pltpu.HBM)
    basis_in = pltpu.with_memory_space_constraint(proj_basis, pltpu.HBM)
    own, s1, s2, s3 = call(
        project_body,
        [((toks, rank), f32)] + [((toks, rank), bf16)] * 3,
        2,
        scratch=[
            pltpu.VMEM((NX, tokens, width // NX), bf16),
            pltpu.VMEM((width, rank), bf16),
            pltpu.VMEM((tokens, rank), f32),
            pltpu.SemaphoreType.DMA((2 * NX,)),
        ],
        in_specs=[HBM] * 2,
        limit=16,
    )(features, basis_in)
    r2, r1, r3 = to_x(s2, 2), to_x(s1, 1), to_x(s3, 3)

    block = (NY, NZ, rows, tokens)
    wide = NZ * NC * rows
    keep, *sends, basis_t = call(
        turn_body,
        [(block, bf16)] + [((NY // SPLIT, NZ, rows, tokens), bf16)] * SPLIT + [((rank, width), bf16)],
        3,
        scratch=[
            pltpu.VMEM((NY, tokens, wide), bf16),
            pltpu.VMEM((width, rank), bf16),
            pltpu.VMEM((wide, tokens), bf16),
            pltpu.SemaphoreType.DMA((NY + 1,)),
        ],
        in_specs=[HBM, HBM, ANY],
    )(grads_in, basis_in, own)
    total, sent = call(sum_x_body, [((toks, rank), f32), ((toks, rank), bf16)], 4)(own, r1, r3, r2)
    half_sum = to_h(sent)
    other = [to_core(a) for a in sends]
    p0 = call(sum_h_body, [((toks, rank), bf16)], 2)(total, half_sum)[0]
    p2, p1, p3 = to_x(p0, 2), to_x(p0, 1), to_x(p0, 3)
    q = to_core(jnp.concatenate([p0, p1, p2, p3], axis=0))

    acc = call(low_own_body, [((NY, NZ * rows, rank), f32)], 5)(keep, p0, p1, p2, p3)[0]
    one, four = (rows, rank), (NY * rows, rank)

    def low_far(rz):
        return call(functools.partial(low_far_body, rz), [(one, f32)] + [(one, bf16)] * 3, 2 + SPLIT)(
            acc, q, *other
        )

    def over_y(s1, s2, s3):
        r2, r1, r3 = to_y(s2, 2), to_y(s1, 1), to_y(s3, 3)
        return r1, r2, r3

    own3, *far3 = low_far(3)
    far3 = over_y(*far3)
    def low_near(rz, dtype):
        return call(functools.partial(low_near_body, rz), [(four, dtype)], 2 + SPLIT)(acc, q, *other)[0]

    send = to_z(low_near(1, bf16), 1)
    near = low_near(0, f32)
    own2, *far2 = low_far(2)
    far2 = over_y(*far2)
    z3 = to_z(call(sum_far_body, [(one, bf16)], 4)(own3, *far3)[0], 3)
    z2 = to_z(call(sum_far_body, [(one, bf16)], 4)(own2, *far2)[0], 2)
    own, y1, y2, y3 = call(sum_near_body, [(one, f32)] + [(one, bf16)] * 3, 2)(near, send)
    y1, y2, y3 = over_y(y1, y2, y3)
    grad, d0 = call(direction_body, [(one, f32), (one, bf16)], 8)(
        z3, z2, own, y1, y2, y3, first_moment, second_moment
    )
    e0 = to_h(d0)
    d2, d1, d3 = to_x(d0, 2), to_x(d0, 1), to_x(d0, 3)
    update = update_part([(0, 0)], [d0], basis_t, None)
    e0, update = lax.optimization_barrier((e0, update))
    e2, e1, e3 = to_x(e0, 2), to_x(e0, 1), to_x(e0, 3)
    grad, _ = lax.optimization_barrier((grad, e0))
    first_new, second_new = call(moments_body, [((1, rows, rank), f32)] * 2, 3)(
        grad, first_moment, second_moment
    )
    update = update_part([(1, 0), (2, 0), (3, 0), (0, 1)], [d1, d2, d3, e0], basis_t, update)
    update = update_part([(1, 1), (2, 1), (3, 1)], [e1, e2, e3], basis_t, update)
    return (update, first_new, second_new)


def solution(mesh):
    return jax.shard_map(
        per_device,
        mesh=mesh,
        in_specs=(
            P("dp", "shard"),
            P("dp", "shard"),
            P("shard", None),
            P("shard", "dp", None),
            P("shard", "dp", None),
        ),
        out_specs=(P(None, "dp", "shard"), P("shard", "dp", None), P("shard", "dp", None)),
        check_vma=False,
    )
```

```python
import functools

import jax
import jax.numpy as jnp
from jax import lax
from jax.experimental import pallas as pl
from jax.experimental.pallas import tpu as pltpu
from jax.sharding import PartitionSpec as P

beta_first = 0.9
beta_second = 0.99
correct_first = 0.9999734386011124
correct_second = 0.6339676587267705
epsilon = 1e-08
galore_scale = 4.0

bf16, f32 = jnp.bfloat16, jnp.float32
NY, NZ, NC, NX, NH = 4, 4, 2, 4, 2
SPLIT = 2
VMEM = pl.BlockSpec(memory_space=pltpu.VMEM)
ANY = pl.BlockSpec(memory_space=pl.ANY)
HBM = pl.BlockSpec(memory_space=pltpu.HBM)


def dp_perm(step):
    pairs = []
    for y in range(NY):
        for z in range(NZ):
            for c in range(NC):
                ty, tz, tc = step(y, z, c)
                pairs.append(((y * NZ + z) * NC + c, ((ty % NY) * NZ + tz) * NC + tc))
    return pairs


def shard_perm(step):
    pairs = []
    for x in range(NX):
        for h in range(NH):
            tx, th = step(x, h)
            pairs.append((x * NH + h, (tx % NX) * NH + th))
    return pairs


def to_core(a):
    return lax.ppermute(a, "dp", dp_perm(lambda y, z, c: (y, z, 1 - c)))


def to_y(a, k):
    return lax.ppermute(a, "dp", dp_perm(lambda y, z, c: (y + k, z, c)))


def to_z(a, k):
    return lax.ppermute(a, "dp", dp_perm(lambda y, z, c: (y, z ^ k, c)))


def to_x(a, k):
    return lax.ppermute(a, "shard", shard_perm(lambda x, h: (x + k, h)))


def to_h(a):
    return lax.ppermute(a, "shard", shard_perm(lambda x, h: (x, 1 - h)))


def place():
    dp, shard = lax.axis_index("dp"), lax.axis_index("shard")
    return dp // (NZ * NC), (dp // NC) % NZ, dp % NC, shard // NH, shard % NH


def call(body, outs, n_in, scratch=(), limit=16, **kw):
    return pl.pallas_call(
        body,
        out_shape=[jax.ShapeDtypeStruct(s, d) for s, d in outs],
        in_specs=kw.pop("in_specs", [VMEM] * n_in),
        out_specs=kw.pop("out_specs", [VMEM] * len(outs)),
        scratch_shapes=list(scratch),
        compiler_params=pltpu.CompilerParams(vmem_limit_bytes=limit << 20),
        **kw,
    )


def project_body(feat, basis, own, s1, s2, s3, fbuf, bbuf, acc, sems):
    _, _, _, x, _ = place()
    rows = own.shape[0]
    part = basis.shape[0] // NX
    copies = []
    for i in range(NX):
        cut = pl.ds(i * part, part)
        copies.append(pltpu.make_async_copy(basis.at[cut, :], bbuf.at[cut, :], sems.at[NX + i]))
        copies.append(pltpu.make_async_copy(feat.at[:, cut], fbuf.at[i], sems.at[i]))
    for copy in copies:
        copy.start()
    for i in range(NX):
        copies[2 * i].wait()
        copies[2 * i + 1].wait()
        t = jnp.dot(fbuf[i], bbuf[i * part : (i + 1) * part, :], preferred_element_type=f32)
        acc[...] = t if i == 0 else acc[...] + t
    for k, out in ((1, s1), (3, s3), (2, s2), (0, own)):
        start = pl.multiple_of(lax.rem(x + k, NX) * rows, rows)
        out[...] = acc[pl.ds(start, rows), :].astype(out.dtype)


def turn_body(grads, basis, _, keep, *refs):
    sends = refs[:SPLIT]
    basis_t, gbuf, bbuf, tmp, sems = refs[SPLIT:]
    y, z, c, x, _ = place()
    rows = keep.shape[2]
    wide = NZ * NC * rows
    toks = gbuf.shape[1] // NX
    copies = []
    for ry in range(NY):
        col = pl.multiple_of(lax.rem(y + ry, NY) * wide, 128)
        copies.append(pltpu.make_async_copy(grads.at[:, pl.ds(col, wide)], gbuf.at[ry], sems.at[ry]))
    copies.append(pltpu.make_async_copy(basis, bbuf, sems.at[NY]))
    for copy in copies:
        copy.start()
    for ry in range(NY):
        copies[ry].wait()
        for k in range(NX):
            tok = pl.multiple_of(lax.rem(x + NX - k, NX) * toks, toks)
            tmp[:, k * toks : (k + 1) * toks] = gbuf[ry, pl.ds(tok, toks), :].T
        for rz in range(NZ):
            base = (z ^ rz) * NC
            keep[ry, rz] = tmp[pl.ds(pl.multiple_of((base + c) * rows, 16), rows), :]
            other = tmp[pl.ds(pl.multiple_of((base + 1 - c) * rows, 16), rows), :]
            sends[ry * SPLIT // NY][ry % (NY // SPLIT), rz] = other
    copies[NY].wait()
    basis_t[...] = bbuf[...].T


def sum_x_body(own, r1, r2, r3, total, sent):
    t = own[...] + r1[...].astype(f32) + r2[...].astype(f32) + r3[...].astype(f32)
    total[...] = t
    sent[...] = t.astype(bf16)


def sum_h_body(own, other, out):
    out[...] = (own[...] + other[...].astype(f32)).astype(bf16)


def low_own_body(keep, p0, p1, p2, p3, acc):
    rows, toks = keep.shape[1] * keep.shape[2], keep.shape[3]
    proj = jnp.concatenate([p[...] for p in (p0, p1, p2, p3)], axis=0)
    for ry in range(NY):
        a = keep[ry].reshape(rows, toks)
        acc[ry] = jnp.dot(a, proj, preferred_element_type=f32)


def low_far_body(rz, acc, q, *refs):
    other, outs = refs[:SPLIT], refs[SPLIT:]
    rows = other[0].shape[2]
    for ry in (2, 1, 3, 0):
        t = acc[ry, rz * rows : (rz + 1) * rows, :]
        t = t + jnp.dot(other[ry * SPLIT // NY][ry % (NY // SPLIT), rz], q[...], preferred_element_type=f32)
        outs[ry][...] = t.astype(outs[ry].dtype)


def low_near_body(rz, acc, q, *refs):
    other, out = refs[:SPLIT], refs[SPLIT]
    rows = other[0].shape[2]
    for ry in range(NY):
        t = acc[ry, rz * rows : (rz + 1) * rows, :]
        t = t + jnp.dot(other[ry * SPLIT // NY][ry % (NY // SPLIT), rz], q[...], preferred_element_type=f32)
        out[ry * rows : (ry + 1) * rows, :] = t.astype(out.dtype)


def low_rest_body(rz, acc, q, *refs):
    low_near_body(0, acc, q, *refs[: SPLIT + 1])
    low_far_body(rz, acc, q, *refs[:SPLIT], *refs[SPLIT + 1 :])


def sum_far_body(own, r1, r2, r3, *refs):
    out = refs[-1]
    t = own[...] + r1[...].astype(f32) + r2[...].astype(f32) + r3[...].astype(f32)
    out[...] = t.astype(out.dtype)


def sum_near_body(own, near, total, s1, s2, s3):
    rows = total.shape[0]
    for ry, out in ((2, s2), (1, s1), (3, s3), (0, total)):
        part = slice(ry * rows, (ry + 1) * rows)
        out[...] = (own[part, :] + near[part, :].astype(f32)).astype(out.dtype)


def direction_body(z3, own, y1, y2, y3, z2, first, second, grad, direction):
    g = own[...] + y1[...].astype(f32) + y2[...].astype(f32) + y3[...].astype(f32)
    g = g + z2[...].astype(f32) + z3[...].astype(f32)
    grad[...] = g
    m = beta_first * first[0] + (1.0 - beta_first) * g
    v = beta_second * second[0] + (1.0 - beta_second) * g * g
    d = m / correct_first / (jnp.sqrt(v / correct_second) + epsilon)
    direction[...] = d.astype(bf16)


def moments_body(grad, first, second, first_new, second_new):
    g = grad[...]
    first_new[0] = beta_first * first[0] + (1.0 - beta_first) * g
    second_new[0] = beta_second * second[0] + (1.0 - beta_second) * g * g


def update_body(moves, aliased, *refs):
    n = len(moves)
    dirs, basis_t = refs[:n], refs[n]
    out, buf, sems = refs[n + 1 + aliased :]
    _, _, _, x, h = place()
    rows, cols = buf.shape[1], buf.shape[2] // 2
    cat = jnp.concatenate([d[...] for d in dirs], axis=0)
    copies = []
    for half in range(2):
        part = slice(half * cols, (half + 1) * cols)
        t = galore_scale * jnp.dot(cat, basis_t[:, part], preferred_element_type=f32)
        for i, (k, flip) in enumerate(moves):
            buf[i, :, part] = t[i * rows : (i + 1) * rows, :].astype(bf16)
            block = lax.rem(x + NX - k, NX) * NH + (h ^ flip)
            cut = pl.ds(half * cols, cols)
            copy = pltpu.make_async_copy(
                buf.at[i, :, cut], out.at[block, :, cut], sems.at[half * n + i]
            )
            copy.start()
            copies.append(copy)
    for copy in copies:
        copy.wait()


def update_part(moves, dirs, basis_t, out):
    n = len(moves)
    rows, rank = dirs[0].shape
    cols = basis_t.shape[1]
    aliased = 0 if out is None else 1
    args = (*dirs, basis_t) + ((out,) if aliased else ())
    return call(
        functools.partial(update_body, moves, aliased),
        [((NX * NH, rows, cols), bf16)],
        len(args),
        scratch=[pltpu.VMEM((n, rows, cols), bf16), pltpu.SemaphoreType.DMA((2 * n,))],
        in_specs=[VMEM] * (n + 1) + [ANY] * aliased,
        out_specs=[ANY],
        input_output_aliases={n + 1: 0} if aliased else {},
    )(*args)[0]


def per_device(features, out_grads, proj_basis, first_moment, second_moment):
    tokens, _ = features.shape
    width, rank = proj_basis.shape
    rows = first_moment.shape[1]
    toks = tokens // NX

    features = pltpu.with_memory_space_constraint(features, pltpu.HBM)
    grads_in = pltpu.with_memory_space_constraint(out_grads, pltpu.HBM)
    basis_in = pltpu.with_memory_space_constraint(proj_basis, pltpu.HBM)
    own, s1, s2, s3 = call(
        project_body,
        [((toks, rank), f32)] + [((toks, rank), bf16)] * 3,
        2,
        scratch=[
            pltpu.VMEM((NX, tokens, width // NX), bf16),
            pltpu.VMEM((width, rank), bf16),
            pltpu.VMEM((tokens, rank), f32),
            pltpu.SemaphoreType.DMA((2 * NX,)),
        ],
        in_specs=[HBM] * 2,
        limit=16,
    )(features, basis_in)
    r2, r1, r3 = to_x(s2, 2), to_x(s1, 1), to_x(s3, 3)

    block = (NY, NZ, rows, tokens)
    wide = NZ * NC * rows
    keep, *sends, basis_t = call(
        turn_body,
        [(block, bf16)] + [((NY // SPLIT, NZ, rows, tokens), bf16)] * SPLIT + [((rank, width), bf16)],
        3,
        scratch=[
            pltpu.VMEM((NY, tokens, wide), bf16),
            pltpu.VMEM((width, rank), bf16),
            pltpu.VMEM((wide, tokens), bf16),
            pltpu.SemaphoreType.DMA((NY + 1,)),
        ],
        in_specs=[HBM, HBM, ANY],
    )(grads_in, basis_in, own)
    total, sent = call(sum_x_body, [((toks, rank), f32), ((toks, rank), bf16)], 4)(own, r1, r3, r2)
    half_sum = to_h(sent)
    other = [to_core(a) for a in sends]
    p0 = call(sum_h_body, [((toks, rank), bf16)], 2)(total, half_sum)[0]
    p2, p1, p3 = to_x(p0, 2), to_x(p0, 1), to_x(p0, 3)
    q = to_core(jnp.concatenate([p0, p1, p2, p3], axis=0))

    acc = call(low_own_body, [((NY, NZ * rows, rank), f32)], 5)(keep, p0, p1, p2, p3)[0]
    one, four = (rows, rank), (NY * rows, rank)

    def low_far(rz):
        return call(functools.partial(low_far_body, rz), [(one, f32)] + [(one, bf16)] * 3, 2 + SPLIT)(
            acc, q, *other
        )

    def over_y(s1, s2, s3):
        r2, r1, r3 = to_y(s2, 2), to_y(s1, 1), to_y(s3, 3)
        return r1, r2, r3

    own3, *far3 = low_far(3)
    far3 = over_y(*far3)
    send = call(functools.partial(low_near_body, 1), [(four, bf16)], 2 + SPLIT)(acc, q, *other)[0]
    send = to_z(send, 1)
    near, own2, *far2 = call(
        functools.partial(low_rest_body, 2), [(four, f32), (one, f32)] + [(one, bf16)] * 3, 2 + SPLIT
    )(acc, q, *other)
    far2 = over_y(*far2)
    z3 = to_z(call(sum_far_body, [(one, bf16)], 4)(own3, *far3)[0], 3)
    z2 = call(sum_far_body, [(one, bf16)], 5, in_specs=[VMEM] * 4 + [ANY])(own2, *far2, send)[0]
    z2 = to_z(z2, 2)
    own, y1, y2, y3 = call(sum_near_body, [(one, f32)] + [(one, bf16)] * 3, 2)(near, send)
    y1, y2, y3 = over_y(y1, y2, y3)
    grad, d0 = call(direction_body, [(one, f32), (one, bf16)], 8)(
        z3, own, y1, y2, y3, z2, first_moment, second_moment
    )
    e0 = to_h(d0)
    d2, d1, d3 = to_x(d0, 2), to_x(d0, 1), to_x(d0, 3)
    update = update_part([(0, 0)], [d0], basis_t, None)
    e0, update = lax.optimization_barrier((e0, update))
    e2, e1, e3 = to_x(e0, 2), to_x(e0, 1), to_x(e0, 3)
    grad, _ = lax.optimization_barrier((grad, e0))
    first_new, second_new = call(moments_body, [((1, rows, rank), f32)] * 2, 3)(
        grad, first_moment, second_moment
    )
    update = update_part([(1, 0), (2, 0), (3, 0), (0, 1)], [d1, d2, d3, e0], basis_t, update)
    update = update_part([(1, 1), (2, 1), (3, 1)], [e1, e2, e3], basis_t, update)
    return (update, first_new, second_new)


def solution(mesh):
    return jax.shard_map(
        per_device,
        mesh=mesh,
        in_specs=(
            P("dp", "shard"),
            P("dp", "shard"),
            P("shard", None),
            P("shard", "dp", None),
            P("shard", "dp", None),
        ),
        out_specs=(P(None, "dp", "shard"), P("shard", "dp", None), P("shard", "dp", None)),
        check_vma=False,
    )
```

```python
import functools

import jax
import jax.numpy as jnp
from jax import lax
from jax.experimental import pallas as pl
from jax.experimental.pallas import tpu as pltpu
from jax.sharding import PartitionSpec as P

beta_first = 0.9
beta_second = 0.99
correct_first = 0.9999734386011124
correct_second = 0.6339676587267705
epsilon = 1e-08
galore_scale = 4.0

bf16, f32 = jnp.bfloat16, jnp.float32
NY, NZ, NC, NX, NH = 4, 4, 2, 4, 2
SPLIT = 2
VMEM = pl.BlockSpec(memory_space=pltpu.VMEM)
ANY = pl.BlockSpec(memory_space=pl.ANY)
HBM = pl.BlockSpec(memory_space=pltpu.HBM)


def dp_perm(step):
    pairs = []
    for y in range(NY):
        for z in range(NZ):
            for c in range(NC):
                ty, tz, tc = step(y, z, c)
                pairs.append(((y * NZ + z) * NC + c, ((ty % NY) * NZ + tz) * NC + tc))
    return pairs


def shard_perm(step):
    pairs = []
    for x in range(NX):
        for h in range(NH):
            tx, th = step(x, h)
            pairs.append((x * NH + h, (tx % NX) * NH + th))
    return pairs


def to_core(a):
    return lax.ppermute(a, "dp", dp_perm(lambda y, z, c: (y, z, 1 - c)))


def to_y(a, k):
    return lax.ppermute(a, "dp", dp_perm(lambda y, z, c: (y + k, z, c)))


def to_z(a, k):
    return lax.ppermute(a, "dp", dp_perm(lambda y, z, c: (y, z ^ k, c)))


def to_x(a, k):
    return lax.ppermute(a, "shard", shard_perm(lambda x, h: (x + k, h)))


def to_h(a):
    return lax.ppermute(a, "shard", shard_perm(lambda x, h: (x, 1 - h)))


def place():
    dp, shard = lax.axis_index("dp"), lax.axis_index("shard")
    return dp // (NZ * NC), (dp // NC) % NZ, dp % NC, shard // NH, shard % NH


def call(body, outs, n_in, scratch=(), limit=16, **kw):
    return pl.pallas_call(
        body,
        out_shape=[jax.ShapeDtypeStruct(s, d) for s, d in outs],
        in_specs=kw.pop("in_specs", [VMEM] * n_in),
        out_specs=kw.pop("out_specs", [VMEM] * len(outs)),
        scratch_shapes=list(scratch),
        compiler_params=pltpu.CompilerParams(vmem_limit_bytes=limit << 20),
        **kw,
    )


def project_body(feat, basis, own, s1, s2, s3, fbuf, bbuf, acc, sems):
    _, _, _, x, _ = place()
    rows = own.shape[0]
    part = basis.shape[0] // NX
    copies = []
    for i in range(NX):
        cut = pl.ds(i * part, part)
        copies.append(pltpu.make_async_copy(basis.at[cut, :], bbuf.at[cut, :], sems.at[NX + i]))
        copies.append(pltpu.make_async_copy(feat.at[:, cut], fbuf.at[i], sems.at[i]))
    for copy in copies:
        copy.start()
    for i in range(NX):
        copies[2 * i].wait()
        copies[2 * i + 1].wait()
        t = jnp.dot(fbuf[i], bbuf[i * part : (i + 1) * part, :], preferred_element_type=f32)
        acc[...] = t if i == 0 else acc[...] + t
    for k, out in ((1, s1), (3, s3), (2, s2), (0, own)):
        start = pl.multiple_of(lax.rem(x + k, NX) * rows, rows)
        out[...] = acc[pl.ds(start, rows), :].astype(out.dtype)


def turn_body(grads, basis, _, keep, *refs):
    sends = refs[:SPLIT]
    basis_t, gbuf, bbuf, tmp, sems = refs[SPLIT:]
    y, z, c, x, _ = place()
    rows = keep.shape[2]
    wide = NZ * NC * rows
    toks = gbuf.shape[1] // NX
    copies = []
    for ry in range(NY):
        col = pl.multiple_of(lax.rem(y + ry, NY) * wide, 128)
        copies.append(pltpu.make_async_copy(grads.at[:, pl.ds(col, wide)], gbuf.at[ry], sems.at[ry]))
    copies.append(pltpu.make_async_copy(basis, bbuf, sems.at[NY]))
    for copy in copies:
        copy.start()
    for ry in range(NY):
        copies[ry].wait()
        for k in range(NX):
            tok = pl.multiple_of(lax.rem(x + NX - k, NX) * toks, toks)
            tmp[:, k * toks : (k + 1) * toks] = gbuf[ry, pl.ds(tok, toks), :].T
        for rz in range(NZ):
            base = (z ^ rz) * NC
            keep[ry, rz] = tmp[pl.ds(pl.multiple_of((base + c) * rows, 16), rows), :]
            other = tmp[pl.ds(pl.multiple_of((base + 1 - c) * rows, 16), rows), :]
            sends[ry * SPLIT // NY][ry % (NY // SPLIT), rz] = other
    copies[NY].wait()
    basis_t[...] = bbuf[...].T


def sum_x_body(own, r1, r2, r3, total, sent):
    t = own[...] + r1[...].astype(f32) + r2[...].astype(f32) + r3[...].astype(f32)
    total[...] = t
    sent[...] = t.astype(bf16)


def sum_h_body(own, other, out):
    out[...] = (own[...] + other[...].astype(f32)).astype(bf16)


def low_own_body(keep, p0, p1, p2, p3, acc):
    rows, toks = keep.shape[1] * keep.shape[2], keep.shape[3]
    proj = jnp.concatenate([p[...] for p in (p0, p1, p2, p3)], axis=0)
    for ry in range(NY):
        a = keep[ry].reshape(rows, toks)
        acc[ry] = jnp.dot(a, proj, preferred_element_type=f32)


def low_far_body(rz, acc, q, *refs):
    other, outs = refs[:SPLIT], refs[SPLIT:]
    rows = other[0].shape[2]
    for ry in (2, 1, 3, 0):
        t = acc[ry, rz * rows : (rz + 1) * rows, :]
        t = t + jnp.dot(other[ry * SPLIT // NY][ry % (NY // SPLIT), rz], q[...], preferred_element_type=f32)
        outs[ry][...] = t.astype(outs[ry].dtype)


def low_near_body(rz, acc, q, *refs):
    other, out = refs[:SPLIT], refs[SPLIT]
    rows = other[0].shape[2]
    for ry in range(NY):
        t = acc[ry, rz * rows : (rz + 1) * rows, :]
        t = t + jnp.dot(other[ry * SPLIT // NY][ry % (NY // SPLIT), rz], q[...], preferred_element_type=f32)
        out[ry * rows : (ry + 1) * rows, :] = t.astype(out.dtype)


def low_rest_body(rz, acc, q, *refs):
    low_near_body(0, acc, q, *refs[: SPLIT + 1])
    low_far_body(rz, acc, q, *refs[:SPLIT], *refs[SPLIT + 1 :])


def sum_far_body(own, r1, r2, r3, *refs):
    out = refs[-1]
    t = own[...] + r1[...].astype(f32) + r2[...].astype(f32) + r3[...].astype(f32)
    out[...] = t.astype(out.dtype)


def sum_near_body(parts, own, near, *refs):
    rows = refs[-1].shape[0]
    for ry, out in zip(parts, refs[-len(parts) :]):
        part = slice(ry * rows, (ry + 1) * rows)
        out[...] = (own[part, :] + near[part, :].astype(f32)).astype(out.dtype)


def direction_body(z3, own, y1, y3, z2, y2, first, second, grad, direction):
    g = own[...] + y1[...].astype(f32) + y2[...].astype(f32) + y3[...].astype(f32)
    g = g + z2[...].astype(f32) + z3[...].astype(f32)
    grad[...] = g
    m = beta_first * first[0] + (1.0 - beta_first) * g
    v = beta_second * second[0] + (1.0 - beta_second) * g * g
    d = m / correct_first / (jnp.sqrt(v / correct_second) + epsilon)
    direction[...] = d.astype(bf16)


def moments_body(grad, first, second, first_new, second_new):
    g = grad[...]
    first_new[0] = beta_first * first[0] + (1.0 - beta_first) * g
    second_new[0] = beta_second * second[0] + (1.0 - beta_second) * g * g


def update_body(moves, aliased, *refs):
    n = len(moves)
    dirs, basis_t = refs[:n], refs[n]
    out, buf, sems = refs[n + 1 + aliased :]
    _, _, _, x, h = place()
    rows, cols = buf.shape[1], buf.shape[2] // 2
    cat = jnp.concatenate([d[...] for d in dirs], axis=0)
    copies = []
    for half in range(2):
        part = slice(half * cols, (half + 1) * cols)
        t = galore_scale * jnp.dot(cat, basis_t[:, part], preferred_element_type=f32)
        for i, (k, flip) in enumerate(moves):
            buf[i, :, part] = t[i * rows : (i + 1) * rows, :].astype(bf16)
            block = lax.rem(x + NX - k, NX) * NH + (h ^ flip)
            cut = pl.ds(half * cols, cols)
            copy = pltpu.make_async_copy(
                buf.at[i, :, cut], out.at[block, :, cut], sems.at[half * n + i]
            )
            copy.start()
            copies.append(copy)
    for copy in copies:
        copy.wait()


def update_part(moves, dirs, basis_t, out):
    n = len(moves)
    rows, rank = dirs[0].shape
    cols = basis_t.shape[1]
    aliased = 0 if out is None else 1
    args = (*dirs, basis_t) + ((out,) if aliased else ())
    return call(
        functools.partial(update_body, moves, aliased),
        [((NX * NH, rows, cols), bf16)],
        len(args),
        scratch=[pltpu.VMEM((n, rows, cols), bf16), pltpu.SemaphoreType.DMA((2 * n,))],
        in_specs=[VMEM] * (n + 1) + [ANY] * aliased,
        out_specs=[ANY],
        input_output_aliases={n + 1: 0} if aliased else {},
    )(*args)[0]


def per_device(features, out_grads, proj_basis, first_moment, second_moment):
    tokens, _ = features.shape
    width, rank = proj_basis.shape
    rows = first_moment.shape[1]
    toks = tokens // NX

    features = pltpu.with_memory_space_constraint(features, pltpu.HBM)
    grads_in = pltpu.with_memory_space_constraint(out_grads, pltpu.HBM)
    basis_in = pltpu.with_memory_space_constraint(proj_basis, pltpu.HBM)
    own, s1, s2, s3 = call(
        project_body,
        [((toks, rank), f32)] + [((toks, rank), bf16)] * 3,
        2,
        scratch=[
            pltpu.VMEM((NX, tokens, width // NX), bf16),
            pltpu.VMEM((width, rank), bf16),
            pltpu.VMEM((tokens, rank), f32),
            pltpu.SemaphoreType.DMA((2 * NX,)),
        ],
        in_specs=[HBM] * 2,
        limit=16,
    )(features, basis_in)
    r2, r1, r3 = to_x(s2, 2), to_x(s1, 1), to_x(s3, 3)

    block = (NY, NZ, rows, tokens)
    wide = NZ * NC * rows
    keep, *sends, basis_t = call(
        turn_body,
        [(block, bf16)] + [((NY // SPLIT, NZ, rows, tokens), bf16)] * SPLIT + [((rank, width), bf16)],
        3,
        scratch=[
            pltpu.VMEM((NY, tokens, wide), bf16),
            pltpu.VMEM((width, rank), bf16),
            pltpu.VMEM((wide, tokens), bf16),
            pltpu.SemaphoreType.DMA((NY + 1,)),
        ],
        in_specs=[HBM, HBM, ANY],
    )(grads_in, basis_in, own)
    total, sent = call(sum_x_body, [((toks, rank), f32), ((toks, rank), bf16)], 4)(own, r1, r3, r2)
    half_sum = to_h(sent)
    other = [to_core(a) for a in sends]
    p0 = call(sum_h_body, [((toks, rank), bf16)], 2)(total, half_sum)[0]
    p2, p1, p3 = to_x(p0, 2), to_x(p0, 1), to_x(p0, 3)
    q = to_core(jnp.concatenate([p0, p1, p2, p3], axis=0))

    acc = call(low_own_body, [((NY, NZ * rows, rank), f32)], 5)(keep, p0, p1, p2, p3)[0]
    one, four = (rows, rank), (NY * rows, rank)

    def low_far(rz):
        return call(functools.partial(low_far_body, rz), [(one, f32)] + [(one, bf16)] * 3, 2 + SPLIT)(
            acc, q, *other
        )

    def over_y(s1, s2, s3):
        r2, r1, r3 = to_y(s2, 2), to_y(s1, 1), to_y(s3, 3)
        return r1, r2, r3

    own3, *far3 = low_far(3)
    far3 = over_y(*far3)
    send = call(functools.partial(low_near_body, 1), [(four, bf16)], 2 + SPLIT)(acc, q, *other)[0]
    send = to_z(send, 1)
    near, own2, *far2 = call(
        functools.partial(low_rest_body, 2), [(four, f32), (one, f32)] + [(one, bf16)] * 3, 2 + SPLIT
    )(acc, q, *other)
    far2 = over_y(*far2)
    z3 = to_z(call(sum_far_body, [(one, bf16)], 4)(own3, *far3)[0], 3)
    z2 = call(sum_far_body, [(one, bf16)], 5, in_specs=[VMEM] * 4 + [ANY])(own2, *far2, send)[0]
    own, y1, y3 = call(
        functools.partial(sum_near_body, (0, 1, 3)), [(one, f32)] + [(one, bf16)] * 2, 2
    )(near, send)
    y1, y3 = to_y(y1, 1), to_y(y3, 3)
    y2 = call(
        functools.partial(sum_near_body, (2,)), [(one, bf16)], 3, in_specs=[VMEM] * 2 + [ANY]
    )(near, send, z2)[0]
    y2 = to_y(y2, 2)
    z2 = to_z(z2, 2)
    grad, d0 = call(direction_body, [(one, f32), (one, bf16)], 8)(
        z3, own, y1, y3, z2, y2, first_moment, second_moment
    )
    e0 = to_h(d0)
    d2, d1, d3 = to_x(d0, 2), to_x(d0, 1), to_x(d0, 3)
    update = update_part([(0, 0)], [d0], basis_t, None)
    e0, update = lax.optimization_barrier((e0, update))
    e2, e1, e3 = to_x(e0, 2), to_x(e0, 1), to_x(e0, 3)
    grad, _ = lax.optimization_barrier((grad, e0))
    first_new, second_new = call(moments_body, [((1, rows, rank), f32)] * 2, 3)(
        grad, first_moment, second_moment
    )
    update = update_part([(1, 0), (2, 0), (3, 0), (0, 1)], [d1, d2, d3, e0], basis_t, update)
    update = update_part([(1, 1), (2, 1), (3, 1)], [e1, e2, e3], basis_t, update)
    return (update, first_new, second_new)


def solution(mesh):
    return jax.shard_map(
        per_device,
        mesh=mesh,
        in_specs=(
            P("dp", "shard"),
            P("dp", "shard"),
            P("shard", None),
            P("shard", "dp", None),
            P("shard", "dp", None),
        ),
        out_specs=(P(None, "dp", "shard"), P("shard", "dp", None), P("shard", "dp", None)),
        check_vma=False,
    )
```

```python
import functools

import jax
import jax.numpy as jnp
from jax import lax
from jax.experimental import pallas as pl
from jax.experimental.pallas import tpu as pltpu
from jax.sharding import PartitionSpec as P

beta_first = 0.9
beta_second = 0.99
correct_first = 0.9999734386011124
correct_second = 0.6339676587267705
epsilon = 1e-08
galore_scale = 4.0

bf16, f32 = jnp.bfloat16, jnp.float32
NY, NZ, NC, NX, NH = 4, 4, 2, 4, 2
SPLIT = 2
VMEM = pl.BlockSpec(memory_space=pltpu.VMEM)
ANY = pl.BlockSpec(memory_space=pl.ANY)
HBM = pl.BlockSpec(memory_space=pltpu.HBM)


def dp_perm(step):
    pairs = []
    for y in range(NY):
        for z in range(NZ):
            for c in range(NC):
                ty, tz, tc = step(y, z, c)
                pairs.append(((y * NZ + z) * NC + c, ((ty % NY) * NZ + tz) * NC + tc))
    return pairs


def shard_perm(step):
    pairs = []
    for x in range(NX):
        for h in range(NH):
            tx, th = step(x, h)
            pairs.append((x * NH + h, (tx % NX) * NH + th))
    return pairs


def to_core(a):
    return lax.ppermute(a, "dp", dp_perm(lambda y, z, c: (y, z, 1 - c)))


def to_y(a, k):
    return lax.ppermute(a, "dp", dp_perm(lambda y, z, c: (y + k, z, c)))


def to_z(a, k):
    return lax.ppermute(a, "dp", dp_perm(lambda y, z, c: (y, z ^ k, c)))


def to_x(a, k):
    return lax.ppermute(a, "shard", shard_perm(lambda x, h: (x + k, h)))


def to_h(a):
    return lax.ppermute(a, "shard", shard_perm(lambda x, h: (x, 1 - h)))


def place():
    dp, shard = lax.axis_index("dp"), lax.axis_index("shard")
    return dp // (NZ * NC), (dp // NC) % NZ, dp % NC, shard // NH, shard % NH


def call(body, outs, n_in, scratch=(), limit=16, **kw):
    return pl.pallas_call(
        body,
        out_shape=[jax.ShapeDtypeStruct(s, d) for s, d in outs],
        in_specs=kw.pop("in_specs", [VMEM] * n_in),
        out_specs=kw.pop("out_specs", [VMEM] * len(outs)),
        scratch_shapes=list(scratch),
        compiler_params=pltpu.CompilerParams(vmem_limit_bytes=limit << 20),
        **kw,
    )


def project_body(feat, basis, own, s1, s2, s3, fbuf, bbuf, acc, sems):
    _, _, _, x, _ = place()
    rows = own.shape[0]
    part = basis.shape[0] // NX
    copies = []
    for i in range(NX):
        cut = pl.ds(i * part, part)
        copies.append(pltpu.make_async_copy(basis.at[cut, :], bbuf.at[cut, :], sems.at[NX + i]))
        copies.append(pltpu.make_async_copy(feat.at[:, cut], fbuf.at[i], sems.at[i]))
    for copy in copies:
        copy.start()
    for i in range(NX):
        copies[2 * i].wait()
        copies[2 * i + 1].wait()
        t = jnp.dot(fbuf[i], bbuf[i * part : (i + 1) * part, :], preferred_element_type=f32)
        acc[...] = t if i == 0 else acc[...] + t
    for k, out in ((1, s1), (3, s3), (2, s2), (0, own)):
        start = pl.multiple_of(lax.rem(x + k, NX) * rows, rows)
        out[...] = acc[pl.ds(start, rows), :].astype(out.dtype)


def turn_body(grads, basis, _, keep, *refs):
    sends = refs[:SPLIT]
    basis_t, gbuf, bbuf, tmp, sems = refs[SPLIT:]
    y, z, c, x, _ = place()
    rows = keep.shape[2]
    wide = NZ * NC * rows
    toks = gbuf.shape[1] // NX
    copies = []
    for ry in range(NY):
        col = pl.multiple_of(lax.rem(y + ry, NY) * wide, 128)
        copies.append(pltpu.make_async_copy(grads.at[:, pl.ds(col, wide)], gbuf.at[ry], sems.at[ry]))
    copies.append(pltpu.make_async_copy(basis, bbuf, sems.at[NY]))
    for copy in copies:
        copy.start()
    for ry in range(NY):
        copies[ry].wait()
        for k in range(NX):
            tok = pl.multiple_of(lax.rem(x + NX - k, NX) * toks, toks)
            tmp[:, k * toks : (k + 1) * toks] = gbuf[ry, pl.ds(tok, toks), :].T
        for rz in range(NZ):
            base = (z ^ rz) * NC
            keep[ry, rz] = tmp[pl.ds(pl.multiple_of((base + c) * rows, 16), rows), :]
            other = tmp[pl.ds(pl.multiple_of((base + 1 - c) * rows, 16), rows), :]
            sends[ry * SPLIT // NY][ry % (NY // SPLIT), rz] = other
    copies[NY].wait()
    basis_t[...] = bbuf[...].T


def sum_x_body(own, r1, r2, r3, total, sent):
    t = own[...] + r1[...].astype(f32) + r2[...].astype(f32) + r3[...].astype(f32)
    total[...] = t
    sent[...] = t.astype(bf16)


def sum_h_body(own, other, out):
    out[...] = (own[...] + other[...].astype(f32)).astype(bf16)


def low_own_body(keep, p0, p1, p2, p3, acc):
    rows, toks = keep.shape[1] * keep.shape[2], keep.shape[3]
    proj = jnp.concatenate([p[...] for p in (p0, p1, p2, p3)], axis=0)
    for ry in range(NY):
        a = keep[ry].reshape(rows, toks)
        acc[ry] = jnp.dot(a, proj, preferred_element_type=f32)


def low_far_body(rz, acc, q, *refs):
    other, outs = refs[:SPLIT], refs[SPLIT:]
    rows = other[0].shape[2]
    for ry in (2, 1, 3, 0):
        t = acc[ry, rz * rows : (rz + 1) * rows, :]
        t = t + jnp.dot(other[ry * SPLIT // NY][ry % (NY // SPLIT), rz], q[...], preferred_element_type=f32)
        outs[ry][...] = t.astype(outs[ry].dtype)


def low_near_body(rz, acc, q, *refs):
    other, out = refs[:SPLIT], refs[SPLIT]
    rows = other[0].shape[2]
    for ry in range(NY):
        t = acc[ry, rz * rows : (rz + 1) * rows, :]
        t = t + jnp.dot(other[ry * SPLIT // NY][ry % (NY // SPLIT), rz], q[...], preferred_element_type=f32)
        out[ry * rows : (ry + 1) * rows, :] = t.astype(out.dtype)


def low_rest_body(rz, acc, q, *refs):
    low_near_body(0, acc, q, *refs[: SPLIT + 1])
    low_far_body(rz, acc, q, *refs[:SPLIT], *refs[SPLIT + 1 :])


def sum_far_body(own, r1, r2, r3, *refs):
    out = refs[-1]
    t = own[...] + r1[...].astype(f32) + r2[...].astype(f32) + r3[...].astype(f32)
    out[...] = t.astype(out.dtype)


def sum_near_body(parts, own, near, *refs):
    rows = refs[-1].shape[0]
    for ry, out in zip(parts, refs[-len(parts) :]):
        part = slice(ry * rows, (ry + 1) * rows)
        out[...] = (own[part, :] + near[part, :].astype(f32)).astype(out.dtype)


def direction_body(z3, own, y1, y2, z2, y3, first, second, grad, direction):
    g = own[...] + y1[...].astype(f32) + y2[...].astype(f32) + y3[...].astype(f32)
    g = g + z2[...].astype(f32) + z3[...].astype(f32)
    grad[...] = g
    m = beta_first * first[0] + (1.0 - beta_first) * g
    v = beta_second * second[0] + (1.0 - beta_second) * g * g
    d = m / correct_first / (jnp.sqrt(v / correct_second) + epsilon)
    direction[...] = d.astype(bf16)


def moments_body(grad, first, second, first_new, second_new):
    g = grad[...]
    first_new[0] = beta_first * first[0] + (1.0 - beta_first) * g
    second_new[0] = beta_second * second[0] + (1.0 - beta_second) * g * g


def update_body(moves, aliased, *refs):
    n = len(moves)
    dirs, basis_t = refs[:n], refs[n]
    out, buf, sems = refs[n + 1 + aliased :]
    _, _, _, x, h = place()
    rows, cols = buf.shape[1], buf.shape[2] // 2
    cat = jnp.concatenate([d[...] for d in dirs], axis=0)
    copies = []
    for half in range(2):
        part = slice(half * cols, (half + 1) * cols)
        t = galore_scale * jnp.dot(cat, basis_t[:, part], preferred_element_type=f32)
        for i, (k, flip) in enumerate(moves):
            buf[i, :, part] = t[i * rows : (i + 1) * rows, :].astype(bf16)
            block = lax.rem(x + NX - k, NX) * NH + (h ^ flip)
            cut = pl.ds(half * cols, cols)
            copy = pltpu.make_async_copy(
                buf.at[i, :, cut], out.at[block, :, cut], sems.at[half * n + i]
            )
            copy.start()
            copies.append(copy)
    for copy in copies:
        copy.wait()


def update_part(moves, dirs, basis_t, out):
    n = len(moves)
    rows, rank = dirs[0].shape
    cols = basis_t.shape[1]
    aliased = 0 if out is None else 1
    args = (*dirs, basis_t) + ((out,) if aliased else ())
    return call(
        functools.partial(update_body, moves, aliased),
        [((NX * NH, rows, cols), bf16)],
        len(args),
        scratch=[pltpu.VMEM((n, rows, cols), bf16), pltpu.SemaphoreType.DMA((2 * n,))],
        in_specs=[VMEM] * (n + 1) + [ANY] * aliased,
        out_specs=[ANY],
        input_output_aliases={n + 1: 0} if aliased else {},
    )(*args)[0]


def per_device(features, out_grads, proj_basis, first_moment, second_moment):
    tokens, _ = features.shape
    width, rank = proj_basis.shape
    rows = first_moment.shape[1]
    toks = tokens // NX

    features = pltpu.with_memory_space_constraint(features, pltpu.HBM)
    grads_in = pltpu.with_memory_space_constraint(out_grads, pltpu.HBM)
    basis_in = pltpu.with_memory_space_constraint(proj_basis, pltpu.HBM)
    own, s1, s2, s3 = call(
        project_body,
        [((toks, rank), f32)] + [((toks, rank), bf16)] * 3,
        2,
        scratch=[
            pltpu.VMEM((NX, tokens, width // NX), bf16),
            pltpu.VMEM((width, rank), bf16),
            pltpu.VMEM((tokens, rank), f32),
            pltpu.SemaphoreType.DMA((2 * NX,)),
        ],
        in_specs=[HBM] * 2,
        limit=16,
    )(features, basis_in)
    r2, r1, r3 = to_x(s2, 2), to_x(s1, 1), to_x(s3, 3)

    block = (NY, NZ, rows, tokens)
    wide = NZ * NC * rows
    keep, *sends, basis_t = call(
        turn_body,
        [(block, bf16)] + [((NY // SPLIT, NZ, rows, tokens), bf16)] * SPLIT + [((rank, width), bf16)],
        3,
        scratch=[
            pltpu.VMEM((NY, tokens, wide), bf16),
            pltpu.VMEM((width, rank), bf16),
            pltpu.VMEM((wide, tokens), bf16),
            pltpu.SemaphoreType.DMA((NY + 1,)),
        ],
        in_specs=[HBM, HBM, ANY],
    )(grads_in, basis_in, own)
    total, sent = call(sum_x_body, [((toks, rank), f32), ((toks, rank), bf16)], 4)(own, r1, r3, r2)
    half_sum = to_h(sent)
    other = [to_core(a) for a in sends]
    p0 = call(sum_h_body, [((toks, rank), bf16)], 2)(total, half_sum)[0]
    p2, p1, p3 = to_x(p0, 2), to_x(p0, 1), to_x(p0, 3)
    q = to_core(jnp.concatenate([p0, p1, p2, p3], axis=0))

    acc = call(low_own_body, [((NY, NZ * rows, rank), f32)], 5)(keep, p0, p1, p2, p3)[0]
    one, four = (rows, rank), (NY * rows, rank)

    def low_far(rz):
        return call(functools.partial(low_far_body, rz), [(one, f32)] + [(one, bf16)] * 3, 2 + SPLIT)(
            acc, q, *other
        )

    def over_y(s1, s2, s3):
        return to_y(s1, 1), to_y(s3, 3), to_y(s2, 2)

    own3, *far3 = low_far(3)
    far3 = over_y(*far3)
    send = call(functools.partial(low_near_body, 1), [(four, bf16)], 2 + SPLIT)(acc, q, *other)[0]
    send = to_z(send, 1)
    near, own2, *far2 = call(
        functools.partial(low_rest_body, 2), [(four, f32), (one, f32)] + [(one, bf16)] * 3, 2 + SPLIT
    )(acc, q, *other)
    far2 = over_y(*far2)
    z3 = to_z(call(sum_far_body, [(one, bf16)], 4)(own3, *far3)[0], 3)
    z2 = call(sum_far_body, [(one, bf16)], 5, in_specs=[VMEM] * 4 + [ANY])(own2, *far2, send)[0]
    own, y1, y2 = call(
        functools.partial(sum_near_body, (0, 1, 2)), [(one, f32)] + [(one, bf16)] * 2, 2
    )(near, send)
    y1, y2 = to_y(y1, 1), to_y(y2, 2)
    y3 = call(
        functools.partial(sum_near_body, (3,)), [(one, bf16)], 3, in_specs=[VMEM] * 2 + [ANY]
    )(near, send, z2)[0]
    y3 = to_y(y3, 3)
    z2 = to_z(z2, 2)
    grad, d0 = call(direction_body, [(one, f32), (one, bf16)], 8)(
        z3, own, y1, y2, z2, y3, first_moment, second_moment
    )
    e0 = to_h(d0)
    d2, d1, d3 = to_x(d0, 2), to_x(d0, 1), to_x(d0, 3)
    update = update_part([(0, 0)], [d0], basis_t, None)
    e0, update = lax.optimization_barrier((e0, update))
    e2, e1, e3 = to_x(e0, 2), to_x(e0, 1), to_x(e0, 3)
    grad, _ = lax.optimization_barrier((grad, e0))
    first_new, second_new = call(moments_body, [((1, rows, rank), f32)] * 2, 3)(
        grad, first_moment, second_moment
    )
    update = update_part([(1, 0), (2, 0), (3, 0), (0, 1)], [d1, d2, d3, e0], basis_t, update)
    update = update_part([(1, 1), (2, 1), (3, 1)], [e1, e2, e3], basis_t, update)
    return (update, first_new, second_new)


def solution(mesh):
    return jax.shard_map(
        per_device,
        mesh=mesh,
        in_specs=(
            P("dp", "shard"),
            P("dp", "shard"),
            P("shard", None),
            P("shard", "dp", None),
            P("shard", "dp", None),
        ),
        out_specs=(P(None, "dp", "shard"), P("shard", "dp", None), P("shard", "dp", None)),
        check_vma=False,
    )
```

```python
import functools

import jax
import jax.numpy as jnp
from jax import lax
from jax.experimental import pallas as pl
from jax.experimental.pallas import tpu as pltpu
from jax.sharding import PartitionSpec as P

beta_first = 0.9
beta_second = 0.99
correct_first = 0.9999734386011124
correct_second = 0.6339676587267705
epsilon = 1e-08
galore_scale = 4.0

bf16, f32 = jnp.bfloat16, jnp.float32
NY, NZ, NC, NX, NH = 4, 4, 2, 4, 2
SPLIT = 2
VMEM = pl.BlockSpec(memory_space=pltpu.VMEM)
ANY = pl.BlockSpec(memory_space=pl.ANY)
HBM = pl.BlockSpec(memory_space=pltpu.HBM)


def dp_perm(step):
    pairs = []
    for y in range(NY):
        for z in range(NZ):
            for c in range(NC):
                ty, tz, tc = step(y, z, c)
                pairs.append(((y * NZ + z) * NC + c, ((ty % NY) * NZ + tz) * NC + tc))
    return pairs


def shard_perm(step):
    pairs = []
    for x in range(NX):
        for h in range(NH):
            tx, th = step(x, h)
            pairs.append((x * NH + h, (tx % NX) * NH + th))
    return pairs


def to_core(a):
    return lax.ppermute(a, "dp", dp_perm(lambda y, z, c: (y, z, 1 - c)))


def to_y(a, k):
    return lax.ppermute(a, "dp", dp_perm(lambda y, z, c: (y + k, z, c)))


def to_z(a, k):
    return lax.ppermute(a, "dp", dp_perm(lambda y, z, c: (y, z ^ k, c)))


def to_x(a, k):
    return lax.ppermute(a, "shard", shard_perm(lambda x, h: (x + k, h)))


def to_h(a):
    return lax.ppermute(a, "shard", shard_perm(lambda x, h: (x, 1 - h)))


def place():
    dp, shard = lax.axis_index("dp"), lax.axis_index("shard")
    return dp // (NZ * NC), (dp // NC) % NZ, dp % NC, shard // NH, shard % NH


def call(body, outs, n_in, scratch=(), limit=16, **kw):
    return pl.pallas_call(
        body,
        out_shape=[jax.ShapeDtypeStruct(s, d) for s, d in outs],
        in_specs=kw.pop("in_specs", [VMEM] * n_in),
        out_specs=kw.pop("out_specs", [VMEM] * len(outs)),
        scratch_shapes=list(scratch),
        compiler_params=pltpu.CompilerParams(vmem_limit_bytes=limit << 20),
        **kw,
    )


def project_body(feat, basis, own, s1, s2, s3, fbuf, bbuf, acc, sems):
    _, _, _, x, _ = place()
    rows = own.shape[0]
    part = basis.shape[0] // NX
    copies = []
    for i in range(NX):
        cut = pl.ds(i * part, part)
        copies.append(pltpu.make_async_copy(basis.at[cut, :], bbuf.at[cut, :], sems.at[NX + i]))
        copies.append(pltpu.make_async_copy(feat.at[:, cut], fbuf.at[i], sems.at[i]))
    for copy in copies:
        copy.start()
    for i in range(NX):
        copies[2 * i].wait()
        copies[2 * i + 1].wait()
        t = jnp.dot(fbuf[i], bbuf[i * part : (i + 1) * part, :], preferred_element_type=f32)
        acc[...] = t if i == 0 else acc[...] + t
    for k, out in ((1, s1), (3, s3), (2, s2), (0, own)):
        start = pl.multiple_of(lax.rem(x + k, NX) * rows, rows)
        out[...] = acc[pl.ds(start, rows), :].astype(out.dtype)


def turn_body(grads, basis, _, keep, *refs):
    sends = refs[:SPLIT]
    basis_t, gbuf, bbuf, tmp, sems = refs[SPLIT:]
    y, z, c, x, _ = place()
    rows = keep.shape[2]
    wide = NZ * NC * rows
    toks = gbuf.shape[1] // NX
    copies = []
    for ry in range(NY):
        col = pl.multiple_of(lax.rem(y + ry, NY) * wide, 128)
        copies.append(pltpu.make_async_copy(grads.at[:, pl.ds(col, wide)], gbuf.at[ry], sems.at[ry]))
    copies.append(pltpu.make_async_copy(basis, bbuf, sems.at[NY]))
    for copy in copies:
        copy.start()
    for ry in range(NY):
        copies[ry].wait()
        for k in range(NX):
            tok = pl.multiple_of(lax.rem(x + NX - k, NX) * toks, toks)
            tmp[:, k * toks : (k + 1) * toks] = gbuf[ry, pl.ds(tok, toks), :].T
        for rz in range(NZ):
            base = (z ^ rz) * NC
            keep[ry, rz] = tmp[pl.ds(pl.multiple_of((base + c) * rows, 16), rows), :]
            other = tmp[pl.ds(pl.multiple_of((base + 1 - c) * rows, 16), rows), :]
            sends[ry * SPLIT // NY][ry % (NY // SPLIT), rz] = other
    copies[NY].wait()
    basis_t[...] = bbuf[...].T


def sum_x_body(own, r1, r2, r3, total, sent):
    t = own[...] + r1[...].astype(f32) + r2[...].astype(f32) + r3[...].astype(f32)
    total[...] = t
    sent[...] = t.astype(bf16)


def sum_h_body(own, other, out):
    out[...] = (own[...] + other[...].astype(f32)).astype(bf16)


def low_own_body(keep, p0, p1, p2, p3, acc):
    rows, toks = keep.shape[1] * keep.shape[2], keep.shape[3]
    proj = jnp.concatenate([p[...] for p in (p0, p1, p2, p3)], axis=0)
    for ry in range(NY):
        a = keep[ry].reshape(rows, toks)
        acc[ry] = jnp.dot(a, proj, preferred_element_type=f32)


def low_far_body(rz, acc, q, *refs):
    other, outs = refs[:SPLIT], refs[SPLIT:]
    rows = other[0].shape[2]
    for ry in (2, 1, 3, 0):
        t = acc[ry, rz * rows : (rz + 1) * rows, :]
        t = t + jnp.dot(other[ry * SPLIT // NY][ry % (NY // SPLIT), rz], q[...], preferred_element_type=f32)
        outs[ry][...] = t.astype(outs[ry].dtype)


def low_near_body(rz, acc, q, *refs):
    other, out = refs[:SPLIT], refs[SPLIT]
    rows = other[0].shape[2]
    for ry in range(NY):
        t = acc[ry, rz * rows : (rz + 1) * rows, :]
        t = t + jnp.dot(other[ry * SPLIT // NY][ry % (NY // SPLIT), rz], q[...], preferred_element_type=f32)
        out[ry * rows : (ry + 1) * rows, :] = t.astype(out.dtype)


def low_pair_body(near, rz, acc, q, *refs):
    low_near_body(near, acc, q, *refs[: SPLIT + 1])
    low_far_body(rz, acc, q, *refs[:SPLIT], *refs[SPLIT + 1 :])


def sum_far_body(own, r1, r2, r3, *refs):
    out = refs[-1]
    t = own[...] + r1[...].astype(f32) + r2[...].astype(f32) + r3[...].astype(f32)
    out[...] = t.astype(out.dtype)


def sum_near_body(parts, own, near, *refs):
    rows = refs[-1].shape[0]
    for ry, out in zip(parts, refs[-len(parts) :]):
        part = slice(ry * rows, (ry + 1) * rows)
        out[...] = (own[part, :] + near[part, :].astype(f32)).astype(out.dtype)


def direction_body(z3, own, y1, y2, z2, y3, first, second, grad, direction):
    g = own[...] + y1[...].astype(f32) + y2[...].astype(f32) + y3[...].astype(f32)
    g = g + z2[...].astype(f32) + z3[...].astype(f32)
    grad[...] = g
    m = beta_first * first[0] + (1.0 - beta_first) * g
    v = beta_second * second[0] + (1.0 - beta_second) * g * g
    d = m / correct_first / (jnp.sqrt(v / correct_second) + epsilon)
    direction[...] = d.astype(bf16)


def moments_body(grad, first, second, first_new, second_new):
    g = grad[...]
    first_new[0] = beta_first * first[0] + (1.0 - beta_first) * g
    second_new[0] = beta_second * second[0] + (1.0 - beta_second) * g * g


def update_body(moves, aliased, *refs):
    n = len(moves)
    dirs, basis_t = refs[:n], refs[n]
    out, buf, sems = refs[n + 1 + aliased :]
    _, _, _, x, h = place()
    rows, cols = buf.shape[1], buf.shape[2] // 2
    cat = jnp.concatenate([d[...] for d in dirs], axis=0)
    copies = []
    for half in range(2):
        part = slice(half * cols, (half + 1) * cols)
        t = galore_scale * jnp.dot(cat, basis_t[:, part], preferred_element_type=f32)
        for i, (k, flip) in enumerate(moves):
            buf[i, :, part] = t[i * rows : (i + 1) * rows, :].astype(bf16)
            block = lax.rem(x + NX - k, NX) * NH + (h ^ flip)
            cut = pl.ds(half * cols, cols)
            copy = pltpu.make_async_copy(
                buf.at[i, :, cut], out.at[block, :, cut], sems.at[half * n + i]
            )
            copy.start()
            copies.append(copy)
    for copy in copies:
        copy.wait()


def update_part(moves, dirs, basis_t, out):
    n = len(moves)
    rows, rank = dirs[0].shape
    cols = basis_t.shape[1]
    aliased = 0 if out is None else 1
    args = (*dirs, basis_t) + ((out,) if aliased else ())
    return call(
        functools.partial(update_body, moves, aliased),
        [((NX * NH, rows, cols), bf16)],
        len(args),
        scratch=[pltpu.VMEM((n, rows, cols), bf16), pltpu.SemaphoreType.DMA((2 * n,))],
        in_specs=[VMEM] * (n + 1) + [ANY] * aliased,
        out_specs=[ANY],
        input_output_aliases={n + 1: 0} if aliased else {},
    )(*args)[0]


def per_device(features, out_grads, proj_basis, first_moment, second_moment):
    tokens, _ = features.shape
    width, rank = proj_basis.shape
    rows = first_moment.shape[1]
    toks = tokens // NX

    features = pltpu.with_memory_space_constraint(features, pltpu.HBM)
    grads_in = pltpu.with_memory_space_constraint(out_grads, pltpu.HBM)
    basis_in = pltpu.with_memory_space_constraint(proj_basis, pltpu.HBM)
    own, s1, s2, s3 = call(
        project_body,
        [((toks, rank), f32)] + [((toks, rank), bf16)] * 3,
        2,
        scratch=[
            pltpu.VMEM((NX, tokens, width // NX), bf16),
            pltpu.VMEM((width, rank), bf16),
            pltpu.VMEM((tokens, rank), f32),
            pltpu.SemaphoreType.DMA((2 * NX,)),
        ],
        in_specs=[HBM] * 2,
        limit=16,
    )(features, basis_in)
    r2, r1, r3 = to_x(s2, 2), to_x(s1, 1), to_x(s3, 3)

    block = (NY, NZ, rows, tokens)
    wide = NZ * NC * rows
    keep, *sends, basis_t = call(
        turn_body,
        [(block, bf16)] + [((NY // SPLIT, NZ, rows, tokens), bf16)] * SPLIT + [((rank, width), bf16)],
        3,
        scratch=[
            pltpu.VMEM((NY, tokens, wide), bf16),
            pltpu.VMEM((width, rank), bf16),
            pltpu.VMEM((wide, tokens), bf16),
            pltpu.SemaphoreType.DMA((NY + 1,)),
        ],
        in_specs=[HBM, HBM, ANY],
    )(grads_in, basis_in, own)
    total, sent = call(sum_x_body, [((toks, rank), f32), ((toks, rank), bf16)], 4)(own, r1, r3, r2)
    half_sum = to_h(sent)
    other = [to_core(a) for a in sends]
    p0 = call(sum_h_body, [((toks, rank), bf16)], 2)(total, half_sum)[0]
    p2, p1, p3 = to_x(p0, 2), to_x(p0, 1), to_x(p0, 3)
    q = to_core(jnp.concatenate([p0, p1, p2, p3], axis=0))

    acc = call(low_own_body, [((NY, NZ * rows, rank), f32)], 5)(keep, p0, p1, p2, p3)[0]
    one, four = (rows, rank), (NY * rows, rank)

    def low_pair(near, rz, dtype):
        outs = [(four, dtype), (one, f32)] + [(one, bf16)] * 3
        return call(functools.partial(low_pair_body, near, rz), outs, 2 + SPLIT)(acc, q, *other)

    def over_y(s1, s2, s3):
        return to_y(s1, 1), to_y(s3, 3), to_y(s2, 2)

    send, own3, *far3 = low_pair(1, 3, bf16)
    far3 = over_y(*far3)
    send = to_z(send, 1)
    near, own2, *far2 = low_pair(0, 2, f32)
    far2 = over_y(*far2)
    z3 = to_z(call(sum_far_body, [(one, bf16)], 4)(own3, *far3)[0], 3)
    z2 = call(sum_far_body, [(one, bf16)], 5, in_specs=[VMEM] * 4 + [ANY])(own2, *far2, send)[0]
    own, y1, y2 = call(
        functools.partial(sum_near_body, (0, 1, 2)), [(one, f32)] + [(one, bf16)] * 2, 2
    )(near, send)
    y1, y2 = to_y(y1, 1), to_y(y2, 2)
    y3 = call(
        functools.partial(sum_near_body, (3,)), [(one, bf16)], 3, in_specs=[VMEM] * 2 + [ANY]
    )(near, send, z2)[0]
    y3 = to_y(y3, 3)
    z2 = to_z(z2, 2)
    grad, d0 = call(direction_body, [(one, f32), (one, bf16)], 8)(
        z3, own, y1, y2, z2, y3, first_moment, second_moment
    )
    e0 = to_h(d0)
    d2, d1, d3 = to_x(d0, 2), to_x(d0, 1), to_x(d0, 3)
    update = update_part([(0, 0)], [d0], basis_t, None)
    e0, update = lax.optimization_barrier((e0, update))
    e2, e1, e3 = to_x(e0, 2), to_x(e0, 1), to_x(e0, 3)
    grad, _ = lax.optimization_barrier((grad, e0))
    first_new, second_new = call(moments_body, [((1, rows, rank), f32)] * 2, 3)(
        grad, first_moment, second_moment
    )
    update = update_part([(1, 0), (2, 0), (3, 0), (0, 1)], [d1, d2, d3, e0], basis_t, update)
    update = update_part([(1, 1), (2, 1), (3, 1)], [e1, e2, e3], basis_t, update)
    return (update, first_new, second_new)


def solution(mesh):
    return jax.shard_map(
        per_device,
        mesh=mesh,
        in_specs=(
            P("dp", "shard"),
            P("dp", "shard"),
            P("shard", None),
            P("shard", "dp", None),
            P("shard", "dp", None),
        ),
        out_specs=(P(None, "dp", "shard"), P("shard", "dp", None), P("shard", "dp", None)),
        check_vma=False,
    )
```
